32 devices in a mesh: groups: 2 (over x), dp: 2 (over core), tensor: 8 (over z, y).
Axes of the slice: x: 2, y: 2, z: 4, core: 2. Of those that a mesh axis runs over, the one named last changes fastest.
Arguments:
- gate_preactivation: bfloat16 [3072, 16384], P(('groups', 'dp'), 'tensor'), parts along dimension 0, may hold values from -6 to 6
- up_preactivation: bfloat16 [3072, 16384], P(('groups', 'dp'), 'tensor'), parts along dimension 0, may hold values from -6 to 6
- down_matrix: bfloat16 [16384, 8192], P('tensor'), may hold values from -0.0625 to 0.0625
- adapter_input_maps: bfloat16 [16, 64, 16384], P(('dp', 'tensor')), may hold values from -0.046875 to 0.046875
- adapter_output_maps: bfloat16 [16, 64, 8192], P(('dp', 'tensor')), may hold values from -0.75 to 0.75
- row_adapter_index: int32 [3072], P(('groups', 'dp')), parts along dimension 0, may hold values from 0 to 15
- adapter_storage_slot: int32 [16], replicated, may hold values from 0 to 15, each once
Outputs:
- mixed: bfloat16 [3072, 8192], P(('groups', 'dp'), 'tensor'), parts along dimension 0
The draws below stay inside these ranges and needn't reach their ends.
There are 2 independent parts, one for each index of `groups`. The reference program is written for one: setup_inputs(seed, part) draws one part's arguments, and reference() takes and returns one part's arrays. A program takes and returns all parts, laid end to end along the dimension named above; an argument that names none is the same for every part. Nothing has to cross between parts.
Inputs may be any that keep to these rules, and one draw needn't show every extreme that they name: `adapter_storage_slot`: each slot belongs to exactly one adapter.
All inputs are finite; a program needn't handle non-finite values.
Results may differ from the reference program's by a relative error of at most 0.014.
Values may be sent and summed in bfloat16 or wider, within the bound.
A program may use at most 192 MiB of HBM per device.

```python
import math
import jax
import jax.numpy as jnp
import numpy as np
from jax import lax

MODEL_WIDTH = 8192
HIDDEN_UNITS = 16384
ADAPTER_RANK = 64
ROWS = 1536
ADAPTER_TOTAL = 16
N_TENSOR = 8


def place_ends(entries, key, smallest, top_value):
    index_at = [jax.random.randint(jax.random.fold_in(key, axis), (), 0, length) for axis, length in enumerate(entries.shape)]
    longest = entries.shape.index(max(entries.shape))
    neighbour = index_at[:longest] + [(index_at[longest] + 1) % entries.shape[longest]] + index_at[longest + 1:]
    return entries.at[tuple(index_at)].set(smallest).at[tuple(neighbour)].set(top_value)


def raised(entries, stream_key, source, target, blocks, factor):
    owner, partner = [(jnp.arange(entries.shape[axis_at]) // (entries.shape[axis_at] // blocks)).reshape([-1 if axis == axis_at else 1 for axis in range(entries.ndim)]) for axis_at in (source, target)]
    chosen = jax.random.permutation(stream_key, blocks)[partner]
    strong = (owner == chosen) | (owner == (partner + blocks // 2) % blocks)
    return jnp.where(strong, factor * entries, entries)


def steps_of(own_key, extent, pieces, least, largest):
    factor_of, own = 1.0, jax.random.fold_in(own_key, 6)
    for position, shards_of in pieces:
        draws = jnp.exp(jax.random.uniform(jax.random.fold_in(own, position), (shards_of,), jnp.float32, least / len(pieces), largest / len(pieces)))
        factor_of = factor_of * jnp.repeat(draws, extent[position] // shards_of).reshape([-1 if axis == position else 1 for axis in range(len(extent))])
    return factor_of


def cumulative_ranks(number_of, skew):
    weights = [(1 << 20) // math.isqrt(standing ** skew) + 1 for standing in range(1, number_of + 1)]
    deviation = 1 + sum(weights) // (1 << 30)
    return np.cumsum(np.array([max(1, weight // deviation) for weight in weights]))


def ranked_ids(rng, extent, number_of, skew):
    grid = cumulative_ranks(number_of, skew)
    pick = jax.random.randint(jax.random.fold_in(rng, 1), extent, 0, int(grid[number_of - 1]))
    rank = jnp.searchsorted(jnp.asarray(grid, jnp.int32), pick, side="right")
    return jax.random.permutation(jax.random.fold_in(rng, 2), number_of)[rank].astype(jnp.int32)


def scatter_about(stream_key, extent, scale, most, split=(), kind=jnp.bfloat16):
    factor_of = steps_of(stream_key, extent, split, -0.22, 0.18) if split else 1.0
    entries = jax.random.normal(stream_key, extent, jnp.float32) * scale * factor_of
    return jnp.minimum(jnp.maximum(entries, -most), most).astype(kind)


def bell_draw_with(key, dims, scale, bound, cuts, heavy, kind=jnp.bfloat16):
    values = scale * jax.random.normal(key, dims, jnp.float32)
    if cuts:
        values = values * steps_of(key, dims, cuts, -0.22, 0.18)
    return jnp.clip(raised(values, jax.random.fold_in(key, 3), *heavy), -bound, bound).astype(kind)


def setup_inputs(seed: int = 0, part: int = 0) -> dict:
    seeds = jax.random.split(jax.random.key(seed), 8)
    own_keys = jax.random.split(jax.random.fold_in(seeds[7], part), 8)
    gate_preactivation = scatter_about(own_keys[0], (ROWS, HIDDEN_UNITS), 1.0, 6.0, ((0, 2), (1, 8)))
    up_preactivation = scatter_about(own_keys[1], (ROWS, HIDDEN_UNITS), 1.0, 6.0, ((0, 2), (1, 8)))
    down_matrix = bell_draw_with(seeds[2], (HIDDEN_UNITS, MODEL_WIDTH), HIDDEN_UNITS ** -0.5, 0.0625, ((0, 8),), (0, 1, 8, 2.0))
    adapter_input_maps = scatter_about(seeds[3], (ADAPTER_TOTAL, ADAPTER_RANK, HIDDEN_UNITS), HIDDEN_UNITS ** -0.5, 0.046875, ((0, 16),))
    adapter_output_maps = scatter_about(seeds[4], (ADAPTER_TOTAL, ADAPTER_RANK, MODEL_WIDTH), ADAPTER_RANK ** -0.5, 0.75, ((0, 16),))
    row_adapter_index = place_ends(ranked_ids(own_keys[5], (ROWS,), ADAPTER_TOTAL, 2), jax.random.fold_in(own_keys[5], 3), 0, ADAPTER_TOTAL - 1).astype(jnp.int32)
    adapter_storage_slot = jax.random.permutation(seeds[6], ADAPTER_TOTAL).astype(jnp.int32)
    return {"gate_preactivation": gate_preactivation, "up_preactivation": up_preactivation, "down_matrix": down_matrix, "adapter_input_maps": adapter_input_maps, "adapter_output_maps": adapter_output_maps, "row_adapter_index": row_adapter_index, "adapter_storage_slot": adapter_storage_slot}


def reference(gate_preactivation, up_preactivation, down_matrix, adapter_input_maps, adapter_output_maps, row_adapter_index, adapter_storage_slot):
    hidden = (jax.nn.silu(gate_preactivation.astype(jnp.float32)) * up_preactivation.astype(jnp.float32)).astype(jnp.bfloat16)
    block_width = HIDDEN_UNITS // N_TENSOR

    def add_block(total, index):
        start = index * block_width
        piece = lax.dynamic_slice_in_dim(hidden, start, block_width, 1)
        rows_w = lax.dynamic_slice_in_dim(down_matrix, start, block_width, 0)
        partial_sum = jnp.dot(piece, rows_w, preferred_element_type=jnp.float32).astype(jnp.bfloat16)
        partial_sum = lax.optimization_barrier(partial_sum)
        return total + partial_sum.astype(jnp.float32), None

    start_total = jnp.zeros((hidden.shape[0], down_matrix.shape[1]), jnp.float32)
    base, unused = lax.scan(add_block, start_total, jnp.arange(N_TENSOR, dtype=jnp.int32))
    row_storage_slots = adapter_input_maps.shape[0]
    rank_projection = adapter_input_maps.shape[1]
    slot = adapter_storage_slot[row_adapter_index].astype(jnp.int32)
    onehot = (slot[:, None] == jnp.arange(row_storage_slots, dtype=jnp.int32)[None, :])
    flattened_input_maps = adapter_input_maps.reshape(row_storage_slots * rank_projection, adapter_input_maps.shape[2])
    inner = jnp.dot(hidden, flattened_input_maps.T, preferred_element_type=jnp.float32)
    low = jnp.sum(inner.reshape(-1, row_storage_slots, rank_projection) * onehot[:, :, None].astype(jnp.float32), axis=1)
    low_b = low.astype(jnp.bfloat16)
    widened_rows = (onehot[:, :, None].astype(jnp.bfloat16) * low_b[:, None, :]).reshape(-1, row_storage_slots * rank_projection)
    adapter_output = jnp.dot(widened_rows, adapter_output_maps.reshape(row_storage_slots * rank_projection, adapter_output_maps.shape[2]), preferred_element_type=jnp.float32)
    return (base + adapter_output).astype(jnp.bfloat16)
```

```python
import functools

import jax
import jax.numpy as jnp
from jax import lax
from jax.experimental import pallas as pl
from jax.experimental.pallas import tpu as pltpu
from jax.sharding import PartitionSpec as P

MESH = pl.DeviceIdType.MESH
F32, BF16 = jnp.float32, jnp.bfloat16
N_Y, N_Z = 2, 4
CHUNKS = 4
MESSAGES = CHUNKS * N_Z
W_SLOTS = 4
Y_LAG, HOP_LAG = 8, 2
LOW_STEP, SUM_STEP = 8, 11
STEPS = MESSAGES + Y_LAG + HOP_LAG * (N_Z - 1)


def fused(
    gate, up, w, a, b, pos, out,
    hid, part, yrecv, zl, zr, wbuf, stage, aall, ball, lowr, wid,
    y_s, y_r, z_s, zl_r, zr_r, w_sem, st_sem, a_s, a_r, b_s, b_r, l_s, l_r, dp_s, dp_r, own_sem,
):
    tensor = N_Y * N_Z
    t = lax.axis_index("tensor")
    d = lax.axis_index("dp")
    z, y = t // N_Y, t % N_Y
    rows, depth = hid.shape
    block_cols = out.shape[1]
    width = block_cols // CHUNKS
    stage_rows = stage.shape[2]

    def peer(k):
        return lax.rem(t + k, tensor)

    def z_of(m):
        return lax.rem(3 * lax.rem(m, N_Z), N_Z)

    def w_copy(j):
        m, own = j // 2, lax.rem(j, 2)
        y_dest = jnp.where(own == 1, y, 1 - y)
        col = (z_of(m) * N_Y + y_dest) * block_cols + (m // N_Z) * width
        slot = lax.rem(j, W_SLOTS)
        return pltpu.make_async_copy(
            w.at[:, pl.ds(pl.multiple_of(col, width), width)], wbuf.at[slot], w_sem.at[slot]
        )

    def stage_copies(i):
        s = lax.rem(i, 2)
        span = pl.ds(pl.multiple_of(i * stage_rows, stage_rows), stage_rows)
        return [
            pltpu.make_async_copy(src.at[span, :], stage.at[n, s], st_sem.at[n, s])
            for n, src in enumerate((gate, up))
        ]

    def a_copy(source, dest):
        return pltpu.make_async_remote_copy(
            src_ref=a.at[0, :, pl.ds(pl.multiple_of(dest * depth, depth), depth)],
            dst_ref=aall.at[d * tensor + source],
            send_sem=a_s.at[dest], recv_sem=a_r.at[source],
            device_id={"tensor": dest}, device_id_type=MESH,
        )

    def b_copy(source, dest):
        return pltpu.make_async_remote_copy(
            src_ref=b.at[0, :, pl.ds(pl.multiple_of(dest * block_cols, block_cols), block_cols)],
            dst_ref=ball.at[d * tensor + source],
            send_sem=b_s.at[dest], recv_sem=b_r.at[source],
            device_id={"tensor": dest}, device_id_type=MESH,
        )

    def low_copy(source, dest):
        return pltpu.make_async_remote_copy(
            src_ref=lowr.at[source], dst_ref=lowr.at[source],
            send_sem=l_s.at[dest], recv_sem=l_r.at[source],
            device_id={"tensor": dest}, device_id_type=MESH,
        )

    def dp_copy(buf, n, half):
        span = pl.ds(half * tensor, tensor)
        return pltpu.make_async_remote_copy(
            src_ref=buf.at[span], dst_ref=buf.at[span],
            send_sem=dp_s.at[n], recv_sem=dp_r.at[n],
            device_id={"dp": 1 - d}, device_id_type=MESH,
        )

    def y_copy(m):
        return pltpu.make_async_remote_copy(
            src_ref=part.at[0, m], dst_ref=yrecv.at[m],
            send_sem=y_s.at[m], recv_sem=y_r.at[m],
            device_id={"tensor": z * N_Y + 1 - y}, device_id_type=MESH,
        )

    def right_copy(m):
        return pltpu.make_async_remote_copy(
            src_ref=part.at[1, m], dst_ref=zl.at[m],
            send_sem=z_s.at[m], recv_sem=zl_r.at[m],
            device_id={"tensor": lax.rem(t + N_Y, tensor)}, device_id_type=MESH,
        )

    def left_copy(m):
        return pltpu.make_async_remote_copy(
            src_ref=part.at[1, m], dst_ref=zr.at[m],
            send_sem=z_s.at[m], recv_sem=zr_r.at[m],
            device_id={"tensor": lax.rem(t + tensor - N_Y, tensor)}, device_id_type=MESH,
        )

    for copy in stage_copies(0):
        copy.start()

    @pl.loop(0, W_SLOTS)
    def _(j):
        w_copy(j).start()

    own_a = pltpu.make_async_copy(
        a.at[0, :, pl.ds(pl.multiple_of(t * depth, depth), depth)], aall.at[d * tensor + t], own_sem.at[0]
    )
    own_b = pltpu.make_async_copy(
        b.at[0, :, pl.ds(pl.multiple_of(t * block_cols, block_cols), block_cols)],
        ball.at[d * tensor + t], own_sem.at[1],
    )
    own_a.start()
    own_b.start()

    barrier = pltpu.get_barrier_semaphore()

    @pl.loop(1, tensor)
    def _(k):
        pl.semaphore_signal(barrier, inc=1, device_id={"tensor": peer(k)}, device_id_type=MESH)

    pl.semaphore_signal(barrier, inc=1, device_id={"dp": 1 - d}, device_id_type=MESH)
    pl.semaphore_wait(barrier, tensor)

    @pl.loop(1, tensor)
    def _(k):
        a_copy(t, peer(k)).start()

    @pl.loop(0, rows // stage_rows)
    def _(i):
        @pl.when(i + 1 < rows // stage_rows)
        def _():
            for copy in stage_copies(i + 1):
                copy.start()

        for copy in stage_copies(i):
            copy.wait()
        s = lax.rem(i, 2)
        v = stage[0, s].astype(F32)
        u = stage[1, s].astype(F32)
        span = pl.ds(pl.multiple_of(i * stage_rows, stage_rows), stage_rows)
        hid[span, :] = (v / (1.0 + jnp.exp(-v)) * u).astype(BF16)

    def lanes(shape):
        return lax.broadcasted_iota(jnp.int32, shape, 1)

    four = 4 * aall.shape[1]
    pair = 2 * aall.shape[1]
    rank = aall.shape[1]

    def low_of(first, acc):
        def body(q, acc):
            maps = aall[pl.ds(first + 4 * q, 4)].reshape(four, depth)
            inner = lax.dot_general(hid[...], maps, (((1,), (1,)), ((), ())), preferred_element_type=F32)
            wanted = jnp.concatenate([pos[...]] * 2, axis=1) == first + 4 * q + lanes(inner.shape) // rank
            inner = jnp.where(wanted, inner, 0.0)
            return acc + inner[:, :pair] + inner[:, pair:]

        return lax.fori_loop(0, tensor // 4, body, acc)

    half = rows // 2

    @pl.loop(0, STEPS)
    def _(s):
        @pl.when(s < MESSAGES)
        def _():
            @pl.loop(0, 2)
            def _(own):
                j = 2 * s + own
                w_copy(j).wait()
                prod = jnp.dot(hid[...], wbuf[lax.rem(j, W_SLOTS)], preferred_element_type=F32)
                part[own, s] = prod.astype(BF16)

                @pl.when(j + W_SLOTS < 2 * MESSAGES)
                def _():
                    w_copy(j + W_SLOTS).start()

                @pl.when(own == 0)
                def _():
                    y_copy(s).start()

        @pl.when(s == 1)
        def _():
            @pl.loop(1, tensor)
            def _(k):
                b_copy(t, peer(k)).start()

        @pl.when(s == LOW_STEP)
        def _():
            own_a.wait()

            @pl.loop(1, tensor)
            def _(k):
                a_copy(peer(k), t).wait_recv()

            dp_copy(aall, 0, d).start()
            acc = low_of(d * tensor, jnp.zeros((rows, pair), F32))
            dp_copy(aall, 0, 1 - d).wait_recv()
            acc = low_of((1 - d) * tensor, acc)
            both = acc + pltpu.roll(acc, rank, 1)
            lowr[t] = jnp.where(lanes((half, pair)) < rank, both[:half], both[half:]).astype(BF16)

            @pl.loop(1, tensor)
            def _(k):
                low_copy(t, peer(k)).start()

        @pl.when(s == SUM_STEP)
        def _():
            own_b.wait()

            @pl.loop(1, tensor)
            def _(k):
                b_copy(peer(k), t).wait_recv()

            dp_copy(ball, 1, d).start()

            @pl.loop(1, tensor)
            def _(k):
                low_copy(peer(k), t).wait_recv()

            total = lowr[0].astype(F32)
            for k in range(1, tensor):
                total = total + lowr[k].astype(F32)
            total = total.astype(BF16).astype(F32)
            other = pltpu.roll(total, rank, 1)
            low_lane = lanes(total.shape) < rank
            upper = jnp.where(low_lane, total, other)
            lower = jnp.where(low_lane, other, total)
            for k in range(2 * tensor // 2):
                for n, values in enumerate((upper, lower)):
                    span = pl.ds(n * half, half)
                    wanted = pos[span, :] == 2 * k + lanes(values.shape) // rank
                    wid[span, pl.ds(k * pair, pair)] = jnp.where(wanted, values, 0.0).astype(BF16)
            dp_copy(ball, 1, 1 - d).wait_recv()

        mr = s - Y_LAG - HOP_LAG * z

        @pl.when((mr >= 0) & (mr < MESSAGES))
        def _():
            @pl.when(z_of(mr) > z)
            def _():
                y_copy(mr).wait_recv()

                @pl.when(z == 0)
                def _():
                    part[1, mr] = (part[1, mr].astype(F32) + yrecv[mr].astype(F32)).astype(BF16)

                @pl.when(z > 0)
                def _():
                    right_copy(mr).wait_recv()
                    part[1, mr] = (
                        part[1, mr].astype(F32) + yrecv[mr].astype(F32) + zl[mr].astype(F32)
                    ).astype(BF16)

                right_copy(mr).start()

        ml = s - Y_LAG - HOP_LAG * (N_Z - 1 - z)

        @pl.when((ml >= 0) & (ml < MESSAGES))
        def _():
            @pl.when(z_of(ml) < z)
            def _():
                y_copy(ml).wait_recv()

                @pl.when(z == N_Z - 1)
                def _():
                    part[1, ml] = (part[1, ml].astype(F32) + yrecv[ml].astype(F32)).astype(BF16)

                @pl.when(z < N_Z - 1)
                def _():
                    left_copy(ml).wait_recv()
                    part[1, ml] = (
                        part[1, ml].astype(F32) + yrecv[ml].astype(F32) + zr[ml].astype(F32)
                    ).astype(BF16)

                left_copy(ml).start()

        mf = s - Y_LAG - HOP_LAG * jnp.maximum(z, N_Z - 1 - z)

        @pl.when((mf >= 0) & (mf < MESSAGES))
        def _():
            @pl.when(z_of(mf) == z)
            def _():
                y_copy(mf).wait_recv()
                cols = pl.ds(pl.multiple_of((mf // N_Z) * width, width), width)
                maps = ball[:, :, cols].reshape(2 * tensor * rank, width)
                total = jnp.dot(wid[...], maps, preferred_element_type=F32)
                total = total + part[1, mf].astype(F32) + yrecv[mf].astype(F32)

                @pl.when(z == 0)
                def _():
                    left_copy(mf).wait_recv()
                    out[:, cols] = (total + zr[mf].astype(F32)).astype(BF16)

                @pl.when(z == N_Z - 1)
                def _():
                    right_copy(mf).wait_recv()
                    out[:, cols] = (total + zl[mf].astype(F32)).astype(BF16)

                @pl.when((z > 0) & (z < N_Z - 1))
                def _():
                    left_copy(mf).wait_recv()
                    right_copy(mf).wait_recv()
                    out[:, cols] = (total + zl[mf].astype(F32) + zr[mf].astype(F32)).astype(BF16)

    @pl.loop(0, MESSAGES)
    def _(m):
        y_copy(m).wait_send()

        @pl.when(z_of(m) != z)
        def _():
            right_copy(m).wait_send()

    @pl.loop(1, tensor)
    def _(k):
        a_copy(t, peer(k)).wait_send()
        b_copy(t, peer(k)).wait_send()
        low_copy(t, peer(k)).wait_send()

    dp_copy(aall, 0, d).wait_send()
    dp_copy(ball, 1, d).wait_send()


def local_fused(gate, up, w, a, b, row_adapter_index, adapter_storage_slot):
    adapters = adapter_storage_slot.shape[0]
    compare = row_adapter_index[:, None] == jnp.arange(adapters, dtype=jnp.int32)[None, :]
    slot = jnp.sum(jnp.where(compare, adapter_storage_slot[None, :], 0), axis=1)
    tensor = N_Y * N_Z
    rows, depth = gate.shape
    rank = a.shape[1]
    block_cols = w.shape[1] // tensor
    width = block_cols // CHUNKS
    pos = jnp.broadcast_to(slot[:, None], (rows, 2 * rank))
    stage_rows = 64
    hbm = pl.BlockSpec(memory_space=pl.ANY)
    vmem = pl.BlockSpec(memory_space=pltpu.VMEM)
    dma = pltpu.SemaphoreType.DMA
    return pl.pallas_call(
        fused,
        out_shape=jax.ShapeDtypeStruct((rows, block_cols), BF16),
        in_specs=[hbm] * 5 + [vmem],
        out_specs=vmem,
        scratch_shapes=[
            pltpu.VMEM((rows, depth), BF16),
            pltpu.VMEM((2, MESSAGES, rows, width), BF16),
            pltpu.VMEM((MESSAGES, rows, width), BF16),
            pltpu.VMEM((MESSAGES, rows, width), BF16),
            pltpu.VMEM((MESSAGES, rows, width), BF16),
            pltpu.VMEM((W_SLOTS, depth, width), BF16),
            pltpu.VMEM((2, 2, stage_rows, depth), BF16),
            pltpu.VMEM((adapters, rank, depth), BF16),
            pltpu.VMEM((adapters, rank, block_cols), BF16),
            pltpu.VMEM((tensor, rows // 2, 2 * rank), BF16),
            pltpu.VMEM((rows, adapters * rank), BF16),
            dma((MESSAGES,)), dma((MESSAGES,)), dma((MESSAGES,)), dma((MESSAGES,)), dma((MESSAGES,)),
            dma((W_SLOTS,)), dma((2, 2)),
            dma((tensor,)), dma((tensor,)), dma((tensor,)), dma((tensor,)), dma((tensor,)), dma((tensor,)),
            dma((2,)), dma((2,)), dma((2,)),
        ],
        compiler_params=pltpu.CompilerParams(
            collective_id=0, has_side_effects=True, vmem_limit_bytes=60 * 1024 * 1024
        ),
    )(gate, up, w, a, b, pos)


def local(
    gate_preactivation,
    up_preactivation,
    down_matrix,
    adapter_input_maps,
    adapter_output_maps,
    row_adapter_index,
    adapter_storage_slot,
):
    hidden = (
        jax.nn.silu(gate_preactivation.astype(jnp.float32)) * up_preactivation.astype(jnp.float32)
    ).astype(jnp.bfloat16)
    tensor_count = lax.axis_size("tensor")
    data_count = lax.axis_size("dp")
    adapter_count = adapter_storage_slot.shape[0]
    compare = row_adapter_index[:, None] == jnp.arange(adapter_count, dtype=jnp.int32)[None, :]
    slot = jnp.sum(jnp.where(compare, adapter_storage_slot[None, :], 0), axis=1)
    pieces_a, pieces_b = (
        lax.all_gather(adapter_input_maps, "dp", axis=0, tiled=True),
        lax.all_gather(adapter_output_maps, "dp", axis=0, tiled=True),
    )
    pieces_a, pieces_b = (
        lax.all_to_all(pieces_a, "tensor", split_axis=2, concat_axis=0, tiled=True),
        lax.all_to_all(pieces_b, "tensor", split_axis=2, concat_axis=0, tiled=True),
    )
    position = slot % tensor_count * data_count + slot // tensor_count
    row_storage_slots = pieces_a.shape[0]
    rank_projection = pieces_a.shape[1]
    onehot = position[:, None] == jnp.arange(row_storage_slots, dtype=jnp.int32)[None, :]
    flattened_input_maps = pieces_a.reshape(row_storage_slots * rank_projection, pieces_a.shape[2])
    inner = lax.dot_general(
        hidden, flattened_input_maps, (((1,), (1,)), ((), ())), preferred_element_type=jnp.float32
    )
    low_part = jnp.sum(
        inner.reshape(-1, row_storage_slots, rank_projection)
        * onehot[:, :, None].astype(jnp.float32),
        axis=1,
    )
    low_b = lax.psum(low_part.astype(jnp.bfloat16), "tensor")
    widened_rows = (onehot[:, :, None].astype(jnp.bfloat16) * low_b[:, None, :]).reshape(
        -1, row_storage_slots * rank_projection
    )
    adapter_output = jnp.dot(
        widened_rows,
        pieces_b.reshape(row_storage_slots * rank_projection, pieces_b.shape[2]),
        preferred_element_type=jnp.float32,
    )
    partial_out = jnp.dot(hidden, down_matrix, preferred_element_type=jnp.float32)
    base = lax.psum_scatter(
        partial_out.astype(jnp.bfloat16), "tensor", scatter_dimension=1, tiled=True
    ).astype(jnp.float32)
    return (base + adapter_output).astype(jnp.bfloat16)


def solution(mesh):
    placed = (
        P(("groups", "dp"), "tensor"),
        P(("groups", "dp"), "tensor"),
        P("tensor", None),
        P(("dp", "tensor"), None, None),
        P(("dp", "tensor"), None, None),
        P(("groups", "dp")),
        P(),
    )
    sizes = dict(mesh.shape)
    fits = sizes["tensor"] == N_Y * N_Z and sizes["dp"] == 2
    return jax.shard_map(
        local_fused if fits else local, mesh=mesh, in_specs=placed, out_specs=P(("groups", "dp"), "tensor"), check_vma=False
    )
```

```python
import functools

import jax
import jax.numpy as jnp
from jax import lax
from jax.experimental import pallas as pl
from jax.experimental.pallas import tpu as pltpu
from jax.sharding import PartitionSpec as P

MESH = pl.DeviceIdType.MESH
F32, BF16 = jnp.float32, jnp.bfloat16
N_Y, N_Z = 2, 4
CHUNKS = 4
PARTS = 2
MESSAGES = CHUNKS * N_Z * PARTS
W_SLOTS = 4
Y_LAG, HOP_LAG = 10, 3
LOW_STEP, PAIR_STEP, SUM_STEP, FINAL_LAG = 18, 21, 24, 25
STEPS = MESSAGES + FINAL_LAG


def fused(
    gate, up, w, a, b, pos, out,
    hid, part, yrecv, zl, zr, wbuf, stage, aall, ball, lowy, lowz, wid,
    y_s, y_r, z_s, zl_r, zr_r, w_sem, st_sem, a_s, a_r, b_s, b_r, ax_s, ax_r, bx_s, bx_r,
    ly_s, ly_r, lz_s, lz_r, dp_s, dp_r, own_sem,
):
    tensor = N_Y * N_Z
    t = lax.axis_index("tensor")
    d = lax.axis_index("dp")
    g = lax.axis_index("groups")
    z, y = t // N_Y, t % N_Y
    rows, depth = hid.shape
    block_cols = out.shape[1]
    width = block_cols // CHUNKS
    stage_rows = stage.shape[2]
    part_rows = rows // PARTS

    def peer(k):
        return lax.rem(t + k, tensor)

    def z_of(m):
        return lax.rem(3 * lax.rem(m // PARTS, N_Z), N_Z)

    def place(m):
        col = pl.multiple_of(m // (N_Z * PARTS) * width, width)
        row = pl.multiple_of(lax.rem(m, PARTS) * part_rows, part_rows)
        return pl.ds(row, part_rows), pl.ds(col, width)

    rank = aall.shape[1]
    mine = pl.ds(pl.multiple_of(g * (rank // 2), rank // 2), rank // 2)

    def w_copy(j):
        m, own = j // 2 * PARTS, lax.rem(j, 2)
        y_dest = jnp.where(own == 1, y, 1 - y)
        col = (z_of(m) * N_Y + y_dest) * block_cols + m // (N_Z * PARTS) * width
        slot = lax.rem(j, W_SLOTS)
        return pltpu.make_async_copy(
            w.at[:, pl.ds(pl.multiple_of(col, width), width)], wbuf.at[slot], w_sem.at[slot]
        )

    def stage_copies(i):
        s = lax.rem(i, 2)
        span = pl.ds(pl.multiple_of(i * stage_rows, stage_rows), stage_rows)
        return [
            pltpu.make_async_copy(src.at[span, :], stage.at[n, s], st_sem.at[n, s])
            for n, src in enumerate((gate, up))
        ]

    def a_copy(source, dest):
        return pltpu.make_async_remote_copy(
            src_ref=a.at[0, mine, pl.ds(pl.multiple_of(dest * depth, depth), depth)],
            dst_ref=aall.at[d * tensor + source, mine],
            send_sem=a_s.at[dest], recv_sem=a_r.at[source],
            device_id={"tensor": dest}, device_id_type=MESH,
        )

    def b_copy(source, dest):
        return pltpu.make_async_remote_copy(
            src_ref=b.at[0, mine, pl.ds(pl.multiple_of(dest * block_cols, block_cols), block_cols)],
            dst_ref=ball.at[d * tensor + source, mine],
            send_sem=b_s.at[dest], recv_sem=b_r.at[source],
            device_id={"tensor": dest}, device_id_type=MESH,
        )

    def x_copy(buf, send, recv, source, half):
        span = pl.ds(pl.multiple_of(half * (rank // 2), rank // 2), rank // 2)
        return pltpu.make_async_remote_copy(
            src_ref=buf.at[d * tensor + source, span], dst_ref=buf.at[d * tensor + source, span],
            send_sem=send.at[source], recv_sem=recv.at[source],
            device_id={"groups": 1 - g}, device_id_type=MESH,
        )

    def low_y_copy():
        return pltpu.make_async_remote_copy(
            src_ref=lowy.at[0], dst_ref=lowy.at[1], send_sem=ly_s.at[0], recv_sem=ly_r.at[0],
            device_id={"tensor": z * N_Y + 1 - y}, device_id_type=MESH,
        )

    def low_z_copy(source, dest):
        return pltpu.make_async_remote_copy(
            src_ref=lowz.at[source], dst_ref=lowz.at[source],
            send_sem=lz_s.at[dest], recv_sem=lz_r.at[source],
            device_id={"tensor": dest * N_Y + y}, device_id_type=MESH,
        )

    def dp_copy(buf, n, half):
        span = pl.ds(half * tensor, tensor)
        return pltpu.make_async_remote_copy(
            src_ref=buf.at[span], dst_ref=buf.at[span],
            send_sem=dp_s.at[n], recv_sem=dp_r.at[n],
            device_id={"dp": 1 - d}, device_id_type=MESH,
        )

    def y_copy(m):
        return pltpu.make_async_remote_copy(
            src_ref=part.at[0, m], dst_ref=yrecv.at[m],
            send_sem=y_s.at[m], recv_sem=y_r.at[m],
            device_id={"tensor": z * N_Y + 1 - y}, device_id_type=MESH,
        )

    def right_copy(m):
        return pltpu.make_async_remote_copy(
            src_ref=part.at[1, m], dst_ref=zl.at[m],
            send_sem=z_s.at[m], recv_sem=zl_r.at[m],
            device_id={"tensor": lax.rem(t + N_Y, tensor)}, device_id_type=MESH,
        )

    def left_copy(m):
        return pltpu.make_async_remote_copy(
            src_ref=part.at[1, m], dst_ref=zr.at[m],
            send_sem=z_s.at[m], recv_sem=zr_r.at[m],
            device_id={"tensor": lax.rem(t + tensor - N_Y, tensor)}, device_id_type=MESH,
        )

    for copy in stage_copies(0):
        copy.start()

    @pl.loop(0, W_SLOTS)
    def _(j):
        w_copy(j).start()

    own_a = pltpu.make_async_copy(
        a.at[0, mine, pl.ds(pl.multiple_of(t * depth, depth), depth)],
        aall.at[d * tensor + t, mine], own_sem.at[0],
    )
    own_b = pltpu.make_async_copy(
        b.at[0, mine, pl.ds(pl.multiple_of(t * block_cols, block_cols), block_cols)],
        ball.at[d * tensor + t, mine], own_sem.at[1],
    )
    own_a.start()
    own_b.start()

    barrier = pltpu.get_barrier_semaphore()

    @pl.loop(1, tensor)
    def _(k):
        pl.semaphore_signal(barrier, inc=1, device_id={"tensor": peer(k)}, device_id_type=MESH)

    pl.semaphore_signal(barrier, inc=1, device_id={"dp": 1 - d}, device_id_type=MESH)
    pl.semaphore_signal(barrier, inc=1, device_id={"groups": 1 - g}, device_id_type=MESH)
    pl.semaphore_wait(barrier, tensor + 1)

    @pl.loop(1, tensor)
    def _(k):
        a_copy(t, peer(k)).start()

    @pl.loop(1, tensor)
    def _(k):
        b_copy(t, peer(k)).start()

    @pl.loop(0, rows // stage_rows)
    def _(i):
        @pl.when(i + 1 < rows // stage_rows)
        def _():
            for copy in stage_copies(i + 1):
                copy.start()

        for copy in stage_copies(i):
            copy.wait()
        s = lax.rem(i, 2)
        v = stage[0, s].astype(F32)
        u = stage[1, s].astype(F32)
        span = pl.ds(pl.multiple_of(i * stage_rows, stage_rows), stage_rows)
        hid[span, :] = (v / (1.0 + jnp.exp(-v)) * u).astype(BF16)

    def lanes(shape):
        return lax.broadcasted_iota(jnp.int32, shape, 1)

    four = 4 * aall.shape[1]
    pair = 2 * aall.shape[1]

    def low_of(first, acc):
        def body(q, acc):
            maps = aall[pl.ds(first + 4 * q, 4)].reshape(four, depth)
            inner = lax.dot_general(hid[...], maps, (((1,), (1,)), ((), ())), preferred_element_type=F32)
            wanted = jnp.concatenate([pos[...]] * 2, axis=1) == first + 4 * q + lanes(inner.shape) // rank
            inner = jnp.where(wanted, inner, 0.0)
            return acc + inner[:, :pair] + inner[:, pair:]

        return lax.fori_loop(0, tensor // 4, body, acc)

    half = rows // 2

    @pl.loop(0, STEPS)
    def _(s):
        @pl.when((s < MESSAGES) & (lax.rem(s, PARTS) == 0))
        def _():
            @pl.loop(0, 2)
            def _(own):
                j = s // PARTS * 2 + own
                w_copy(j).wait()
                prod = jnp.dot(hid[...], wbuf[lax.rem(j, W_SLOTS)], preferred_element_type=F32)
                part[own, pl.ds(s, PARTS)] = prod.astype(BF16).reshape(PARTS, part_rows, width)

                @pl.when(j + W_SLOTS < 2 * MESSAGES // PARTS)
                def _():
                    w_copy(j + W_SLOTS).start()

                @pl.when(own == 0)
                def _():
                    for n in range(PARTS):
                        y_copy(s + n).start()

        @pl.when(s == 0)
        def _():
            own_a.wait()
            x_copy(aall, ax_s, ax_r, t, g).start()

        @pl.when((s >= 2) & (s < 2 * tensor) & (lax.rem(s, 2) == 0))
        def _():
            source = peer(s // 2)
            a_copy(source, t).wait_recv()
            x_copy(aall, ax_s, ax_r, source, g).start()

        @pl.when(s == LOW_STEP)
        def _():
            own_b.wait()
            x_copy(ball, bx_s, bx_r, t, g).start()

            @pl.loop(1, tensor)
            def _(k):
                b_copy(peer(k), t).wait_recv()
                x_copy(ball, bx_s, bx_r, peer(k), g).start()

            @pl.loop(0, tensor)
            def _(k):
                x_copy(aall, ax_s, ax_r, k, 1 - g).wait_recv()

            dp_copy(aall, 0, d).start()
            acc = low_of(d * tensor, jnp.zeros((rows, pair), F32))
            dp_copy(aall, 0, 1 - d).wait_recv()
            acc = low_of((1 - d) * tensor, acc)
            both = acc + pltpu.roll(acc, rank, 1)
            lowy[0] = jnp.where(lanes((half, pair)) < rank, both[:half], both[half:]).astype(BF16)
            low_y_copy().start()

        @pl.when(s == PAIR_STEP)
        def _():
            low_y_copy().wait_recv()
            lowz[z] = (lowy[0].astype(F32) + lowy[1].astype(F32)).astype(BF16)

            @pl.loop(1, N_Z)
            def _(k):
                low_z_copy(z, lax.rem(z + k, N_Z)).start()

            @pl.loop(0, tensor)
            def _(k):
                x_copy(ball, bx_s, bx_r, k, 1 - g).wait_recv()

            dp_copy(ball, 1, d).start()

        @pl.when(s == SUM_STEP)
        def _():
            @pl.loop(1, N_Z)
            def _(k):
                low_z_copy(lax.rem(z + k, N_Z), z).wait_recv()

            total = lowz[0].astype(F32)
            for k in range(1, N_Z):
                total = total + lowz[k].astype(F32)
            total = total.astype(BF16).astype(F32)
            other = pltpu.roll(total, rank, 1)
            low_lane = lanes(total.shape) < rank
            upper = jnp.where(low_lane, total, other)
            lower = jnp.where(low_lane, other, total)
            for k in range(2 * tensor // 2):
                for n, values in enumerate((upper, lower)):
                    span = pl.ds(n * half, half)
                    wanted = pos[span, :] == 2 * k + lanes(values.shape) // rank
                    wid[span, pl.ds(k * pair, pair)] = jnp.where(wanted, values, 0.0).astype(BF16)
            dp_copy(ball, 1, 1 - d).wait_recv()

        mr = s - Y_LAG - HOP_LAG * z

        @pl.when((mr >= 0) & (mr < MESSAGES))
        def _():
            @pl.when(z_of(mr) > z)
            def _():
                y_copy(mr).wait_recv()

                @pl.when(z == 0)
                def _():
                    part[1, mr] = (part[1, mr].astype(F32) + yrecv[mr].astype(F32)).astype(BF16)

                @pl.when(z > 0)
                def _():
                    right_copy(mr).wait_recv()
                    part[1, mr] = (
                        part[1, mr].astype(F32) + yrecv[mr].astype(F32) + zl[mr].astype(F32)
                    ).astype(BF16)

                right_copy(mr).start()

        ml = s - Y_LAG - HOP_LAG * (N_Z - 1 - z)

        @pl.when((ml >= 0) & (ml < MESSAGES))
        def _():
            @pl.when(z_of(ml) < z)
            def _():
                y_copy(ml).wait_recv()

                @pl.when(z == N_Z - 1)
                def _():
                    part[1, ml] = (part[1, ml].astype(F32) + yrecv[ml].astype(F32)).astype(BF16)

                @pl.when(z < N_Z - 1)
                def _():
                    left_copy(ml).wait_recv()
                    part[1, ml] = (
                        part[1, ml].astype(F32) + yrecv[ml].astype(F32) + zr[ml].astype(F32)
                    ).astype(BF16)

                left_copy(ml).start()

        mf = s - FINAL_LAG

        @pl.when((mf >= 0) & (mf < MESSAGES))
        def _():
            @pl.when(z_of(mf) == z)
            def _():
                y_copy(mf).wait_recv()
                span, cols = place(mf)
                maps = ball[:, :, cols].reshape(2 * tensor * rank, width)
                total = jnp.dot(wid[span, :], maps, preferred_element_type=F32)
                total = total + part[1, mf].astype(F32) + yrecv[mf].astype(F32)

                @pl.when(z == 0)
                def _():
                    left_copy(mf).wait_recv()
                    out[span, cols] = (total + zr[mf].astype(F32)).astype(BF16)

                @pl.when(z == N_Z - 1)
                def _():
                    right_copy(mf).wait_recv()
                    out[span, cols] = (total + zl[mf].astype(F32)).astype(BF16)

                @pl.when((z > 0) & (z < N_Z - 1))
                def _():
                    left_copy(mf).wait_recv()
                    right_copy(mf).wait_recv()
                    out[span, cols] = (total + zl[mf].astype(F32) + zr[mf].astype(F32)).astype(BF16)

    @pl.loop(0, MESSAGES)
    def _(m):
        y_copy(m).wait_send()

        @pl.when(z_of(m) != z)
        def _():
            right_copy(m).wait_send()

    @pl.loop(1, tensor)
    def _(k):
        a_copy(t, peer(k)).wait_send()
        b_copy(t, peer(k)).wait_send()

    @pl.loop(0, tensor)
    def _(k):
        x_copy(aall, ax_s, ax_r, k, g).wait_send()
        x_copy(ball, bx_s, bx_r, k, g).wait_send()

    @pl.loop(1, N_Z)
    def _(k):
        low_z_copy(z, lax.rem(z + k, N_Z)).wait_send()

    low_y_copy().wait_send()
    dp_copy(aall, 0, d).wait_send()
    dp_copy(ball, 1, d).wait_send()


def local_fused(gate, up, w, a, b, row_adapter_index, adapter_storage_slot):
    adapters = adapter_storage_slot.shape[0]
    compare = row_adapter_index[:, None] == jnp.arange(adapters, dtype=jnp.int32)[None, :]
    slot = jnp.sum(jnp.where(compare, adapter_storage_slot[None, :], 0), axis=1)
    tensor = N_Y * N_Z
    rows, depth = gate.shape
    rank = a.shape[1]
    block_cols = w.shape[1] // tensor
    width = block_cols // CHUNKS
    pos = jnp.broadcast_to(slot[:, None], (rows, 2 * rank))
    stage_rows = 64
    hbm = pl.BlockSpec(memory_space=pl.ANY)
    vmem = pl.BlockSpec(memory_space=pltpu.VMEM)
    dma = pltpu.SemaphoreType.DMA
    return pl.pallas_call(
        fused,
        out_shape=jax.ShapeDtypeStruct((rows, block_cols), BF16),
        in_specs=[hbm] * 5 + [vmem],
        out_specs=vmem,
        scratch_shapes=[
            pltpu.VMEM((rows, depth), BF16),
            pltpu.VMEM((2, MESSAGES, rows // PARTS, width), BF16),
            pltpu.VMEM((MESSAGES, rows // PARTS, width), BF16),
            pltpu.VMEM((MESSAGES, rows // PARTS, width), BF16),
            pltpu.VMEM((MESSAGES, rows // PARTS, width), BF16),
            pltpu.VMEM((W_SLOTS, depth, width), BF16),
            pltpu.VMEM((2, 2, stage_rows, depth), BF16),
            pltpu.VMEM((adapters, rank, depth), BF16),
            pltpu.VMEM((adapters, rank, block_cols), BF16),
            pltpu.VMEM((2, rows // 2, 2 * rank), BF16),
            pltpu.VMEM((N_Z, rows // 2, 2 * rank), BF16),
            pltpu.VMEM((rows, adapters * rank), BF16),
            dma((MESSAGES,)), dma((MESSAGES,)), dma((MESSAGES,)), dma((MESSAGES,)), dma((MESSAGES,)),
            dma((W_SLOTS,)), dma((2, 2)),
            dma((tensor,)), dma((tensor,)), dma((tensor,)), dma((tensor,)),
            dma((tensor,)), dma((tensor,)), dma((tensor,)), dma((tensor,)),
            dma((1,)), dma((1,)), dma((N_Z,)), dma((N_Z,)),
            dma((2,)), dma((2,)), dma((2,)),
        ],
        compiler_params=pltpu.CompilerParams(
            collective_id=0, has_side_effects=True, vmem_limit_bytes=60 * 1024 * 1024
        ),
    )(gate, up, w, a, b, pos)


def local(
    gate_preactivation,
    up_preactivation,
    down_matrix,
    adapter_input_maps,
    adapter_output_maps,
    row_adapter_index,
    adapter_storage_slot,
):
    hidden = (
        jax.nn.silu(gate_preactivation.astype(jnp.float32)) * up_preactivation.astype(jnp.float32)
    ).astype(jnp.bfloat16)
    tensor_count = lax.axis_size("tensor")
    data_count = lax.axis_size("dp")
    adapter_count = adapter_storage_slot.shape[0]
    compare = row_adapter_index[:, None] == jnp.arange(adapter_count, dtype=jnp.int32)[None, :]
    slot = jnp.sum(jnp.where(compare, adapter_storage_slot[None, :], 0), axis=1)
    pieces_a, pieces_b = (
        lax.all_gather(adapter_input_maps, "dp", axis=0, tiled=True),
        lax.all_gather(adapter_output_maps, "dp", axis=0, tiled=True),
    )
    pieces_a, pieces_b = (
        lax.all_to_all(pieces_a, "tensor", split_axis=2, concat_axis=0, tiled=True),
        lax.all_to_all(pieces_b, "tensor", split_axis=2, concat_axis=0, tiled=True),
    )
    position = slot % tensor_count * data_count + slot // tensor_count
    row_storage_slots = pieces_a.shape[0]
    rank_projection = pieces_a.shape[1]
    onehot = position[:, None] == jnp.arange(row_storage_slots, dtype=jnp.int32)[None, :]
    flattened_input_maps = pieces_a.reshape(row_storage_slots * rank_projection, pieces_a.shape[2])
    inner = lax.dot_general(
        hidden, flattened_input_maps, (((1,), (1,)), ((), ())), preferred_element_type=jnp.float32
    )
    low_part = jnp.sum(
        inner.reshape(-1, row_storage_slots, rank_projection)
        * onehot[:, :, None].astype(jnp.float32),
        axis=1,
    )
    low_b = lax.psum(low_part.astype(jnp.bfloat16), "tensor")
    widened_rows = (onehot[:, :, None].astype(jnp.bfloat16) * low_b[:, None, :]).reshape(
        -1, row_storage_slots * rank_projection
    )
    adapter_output = jnp.dot(
        widened_rows,
        pieces_b.reshape(row_storage_slots * rank_projection, pieces_b.shape[2]),
        preferred_element_type=jnp.float32,
    )
    partial_out = jnp.dot(hidden, down_matrix, preferred_element_type=jnp.float32)
    base = lax.psum_scatter(
        partial_out.astype(jnp.bfloat16), "tensor", scatter_dimension=1, tiled=True
    ).astype(jnp.float32)
    return (base + adapter_output).astype(jnp.bfloat16)


def solution(mesh):
    placed = (
        P(("groups", "dp"), "tensor"),
        P(("groups", "dp"), "tensor"),
        P("tensor", None),
        P(("dp", "tensor"), None, None),
        P(("dp", "tensor"), None, None),
        P(("groups", "dp")),
        P(),
    )
    sizes = dict(mesh.shape)
    fits = sizes["tensor"] == N_Y * N_Z and sizes["dp"] == 2 and sizes["groups"] == 2
    return jax.shard_map(
        local_fused if fits else local, mesh=mesh, in_specs=placed, out_specs=P(("groups", "dp"), "tensor"), check_vma=False
    )
```

```python
import functools

import jax
import jax.numpy as jnp
from jax import lax
from jax.experimental import pallas as pl
from jax.experimental.pallas import tpu as pltpu
from jax.sharding import PartitionSpec as P

MESH = pl.DeviceIdType.MESH
F32, BF16 = jnp.float32, jnp.bfloat16
N_Y, N_Z = 2, 4
CHUNKS = 4
PARTS = 2
MESSAGES = CHUNKS * N_Z * PARTS
W_SLOTS = 4
Y_LAG, HOP_LAG = 3, 2
LOW_STEP, PAIR_STEP, SUM_STEP, FINAL_LAG = 18, 21, 24, 25
STEPS = MESSAGES + FINAL_LAG


def fused(
    gate, up, w, a, b, pos, out,
    hid, part, yrecv, zl, zr, wbuf, stage, aall, ball, lowy, lowz, wid,
    y_s, y_r, z_s, zl_r, zr_r, w_sem, st_sem, a_s, a_r, b_s, b_r, ax_s, ax_r, bx_s, bx_r,
    ly_s, ly_r, lz_s, lz_r, dp_s, dp_r, own_sem,
):
    tensor = N_Y * N_Z
    t = lax.axis_index("tensor")
    d = lax.axis_index("dp")
    g = lax.axis_index("groups")
    z, y = t // N_Y, t % N_Y
    rows, depth = hid.shape
    block_cols = out.shape[1]
    width = block_cols // CHUNKS
    stage_rows = stage.shape[2]
    part_rows = rows // PARTS

    def peer(k):
        return lax.rem(t + k, tensor)

    def z_of(m):
        return lax.rem(3 * lax.rem(m // PARTS, N_Z), N_Z)

    def place(m):
        col = pl.multiple_of(m // (N_Z * PARTS) * width, width)
        row = pl.multiple_of(lax.rem(m, PARTS) * part_rows, part_rows)
        return pl.ds(row, part_rows), pl.ds(col, width)

    rank = aall.shape[1]
    mine = pl.ds(pl.multiple_of(g * (rank // 2), rank // 2), rank // 2)

    def w_copy(j):
        m, own = j // 2 * PARTS, lax.rem(j, 2)
        y_dest = jnp.where(own == 1, y, 1 - y)
        col = (z_of(m) * N_Y + y_dest) * block_cols + m // (N_Z * PARTS) * width
        slot = lax.rem(j, W_SLOTS)
        return pltpu.make_async_copy(
            w.at[:, pl.ds(pl.multiple_of(col, width), width)], wbuf.at[slot], w_sem.at[slot]
        )

    def stage_copies(i):
        s = lax.rem(i, 2)
        span = pl.ds(pl.multiple_of(i * stage_rows, stage_rows), stage_rows)
        return [
            pltpu.make_async_copy(src.at[span, :], stage.at[n, s], st_sem.at[n, s])
            for n, src in enumerate((gate, up))
        ]

    def a_copy(source, dest):
        return pltpu.make_async_remote_copy(
            src_ref=a.at[0, mine, pl.ds(pl.multiple_of(dest * depth, depth), depth)],
            dst_ref=aall.at[d * tensor + source, mine],
            send_sem=a_s.at[dest], recv_sem=a_r.at[source],
            device_id={"tensor": dest}, device_id_type=MESH,
        )

    def b_copy(source, dest):
        return pltpu.make_async_remote_copy(
            src_ref=b.at[0, mine, pl.ds(pl.multiple_of(dest * block_cols, block_cols), block_cols)],
            dst_ref=ball.at[d * tensor + source, mine],
            send_sem=b_s.at[dest], recv_sem=b_r.at[source],
            device_id={"tensor": dest}, device_id_type=MESH,
        )

    def x_copy(buf, send, recv, source, half):
        span = pl.ds(pl.multiple_of(half * (rank // 2), rank // 2), rank // 2)
        return pltpu.make_async_remote_copy(
            src_ref=buf.at[d * tensor + source, span], dst_ref=buf.at[d * tensor + source, span],
            send_sem=send.at[source], recv_sem=recv.at[source],
            device_id={"groups": 1 - g}, device_id_type=MESH,
        )

    def low_y_copy():
        return pltpu.make_async_remote_copy(
            src_ref=lowy.at[0], dst_ref=lowy.at[1], send_sem=ly_s.at[0], recv_sem=ly_r.at[0],
            device_id={"tensor": z * N_Y + 1 - y}, device_id_type=MESH,
        )

    def low_z_copy(source, dest):
        return pltpu.make_async_remote_copy(
            src_ref=lowz.at[source], dst_ref=lowz.at[source],
            send_sem=lz_s.at[dest], recv_sem=lz_r.at[source],
            device_id={"tensor": dest * N_Y + y}, device_id_type=MESH,
        )

    def dp_copy(buf, n, half):
        span = pl.ds(half * tensor, tensor)
        return pltpu.make_async_remote_copy(
            src_ref=buf.at[span], dst_ref=buf.at[span],
            send_sem=dp_s.at[n], recv_sem=dp_r.at[n],
            device_id={"dp": 1 - d}, device_id_type=MESH,
        )

    def y_copy(m):
        return pltpu.make_async_remote_copy(
            src_ref=part.at[0, m], dst_ref=yrecv.at[m],
            send_sem=y_s.at[m], recv_sem=y_r.at[m],
            device_id={"tensor": z * N_Y + 1 - y}, device_id_type=MESH,
        )

    def right_copy(m):
        return pltpu.make_async_remote_copy(
            src_ref=part.at[1, m], dst_ref=zl.at[m],
            send_sem=z_s.at[m], recv_sem=zl_r.at[m],
            device_id={"tensor": lax.rem(t + N_Y, tensor)}, device_id_type=MESH,
        )

    def left_copy(m):
        return pltpu.make_async_remote_copy(
            src_ref=part.at[1, m], dst_ref=zr.at[m],
            send_sem=z_s.at[m], recv_sem=zr_r.at[m],
            device_id={"tensor": lax.rem(t + tensor - N_Y, tensor)}, device_id_type=MESH,
        )

    for copy in stage_copies(0):
        copy.start()

    @pl.loop(0, W_SLOTS)
    def _(j):
        w_copy(j).start()

    own_a = pltpu.make_async_copy(
        a.at[0, mine, pl.ds(pl.multiple_of(t * depth, depth), depth)],
        aall.at[d * tensor + t, mine], own_sem.at[0],
    )
    own_b = pltpu.make_async_copy(
        b.at[0, mine, pl.ds(pl.multiple_of(t * block_cols, block_cols), block_cols)],
        ball.at[d * tensor + t, mine], own_sem.at[1],
    )
    own_a.start()
    own_b.start()

    barrier = pltpu.get_barrier_semaphore()

    @pl.loop(1, tensor)
    def _(k):
        pl.semaphore_signal(barrier, inc=1, device_id={"tensor": peer(k)}, device_id_type=MESH)

    pl.semaphore_signal(barrier, inc=1, device_id={"dp": 1 - d}, device_id_type=MESH)
    pl.semaphore_signal(barrier, inc=1, device_id={"groups": 1 - g}, device_id_type=MESH)
    pl.semaphore_wait(barrier, tensor + 1)

    @pl.loop(1, tensor)
    def _(k):
        a_copy(t, peer(k)).start()

    @pl.loop(1, tensor)
    def _(k):
        b_copy(t, peer(k)).start()

    @pl.loop(0, rows // stage_rows)
    def _(i):
        @pl.when(i + 1 < rows // stage_rows)
        def _():
            for copy in stage_copies(i + 1):
                copy.start()

        for copy in stage_copies(i):
            copy.wait()
        s = lax.rem(i, 2)
        v = stage[0, s].astype(F32)
        u = stage[1, s].astype(F32)
        span = pl.ds(pl.multiple_of(i * stage_rows, stage_rows), stage_rows)
        hid[span, :] = (v / (1.0 + jnp.exp(-v)) * u).astype(BF16)

    def lanes(shape):
        return lax.broadcasted_iota(jnp.int32, shape, 1)

    four = 4 * aall.shape[1]
    pair = 2 * aall.shape[1]

    def low_of(first, acc):
        def body(q, acc):
            maps = aall[pl.ds(first + 4 * q, 4)].reshape(four, depth)
            inner = lax.dot_general(hid[...], maps, (((1,), (1,)), ((), ())), preferred_element_type=F32)
            wanted = jnp.concatenate([pos[...]] * 2, axis=1) == first + 4 * q + lanes(inner.shape) // rank
            inner = jnp.where(wanted, inner, 0.0)
            return acc + inner[:, :pair] + inner[:, pair:]

        return lax.fori_loop(0, tensor // 4, body, acc)

    half = rows // 2

    @pl.loop(0, STEPS)
    def _(s):
        @pl.when((s < MESSAGES) & (lax.rem(s, PARTS) == 0))
        def _():
            @pl.loop(0, 2)
            def _(own):
                j = s // PARTS * 2 + own
                w_copy(j).wait()
                prod = jnp.dot(hid[...], wbuf[lax.rem(j, W_SLOTS)], preferred_element_type=F32)
                part[own, pl.ds(s, PARTS)] = prod.astype(BF16).reshape(PARTS, part_rows, width)

                @pl.when(j + W_SLOTS < 2 * MESSAGES // PARTS)
                def _():
                    w_copy(j + W_SLOTS).start()

                @pl.when(own == 0)
                def _():
                    for n in range(PARTS):
                        y_copy(s + n).start()

        @pl.when(s == 0)
        def _():
            own_a.wait()
            x_copy(aall, ax_s, ax_r, t, g).start()

        @pl.when((s >= 6) & (s < 6 + tensor - 1))
        def _():
            source = peer(s - 5)
            a_copy(source, t).wait_recv()
            x_copy(aall, ax_s, ax_r, source, g).start()

        @pl.when(s == LOW_STEP)
        def _():
            own_b.wait()
            x_copy(ball, bx_s, bx_r, t, g).start()

            @pl.loop(1, tensor)
            def _(k):
                b_copy(peer(k), t).wait_recv()
                x_copy(ball, bx_s, bx_r, peer(k), g).start()

            @pl.loop(0, tensor)
            def _(k):
                x_copy(aall, ax_s, ax_r, k, 1 - g).wait_recv()

            dp_copy(aall, 0, d).start()
            acc = low_of(d * tensor, jnp.zeros((rows, pair), F32))
            dp_copy(aall, 0, 1 - d).wait_recv()
            acc = low_of((1 - d) * tensor, acc)
            both = acc + pltpu.roll(acc, rank, 1)
            lowy[0] = jnp.where(lanes((half, pair)) < rank, both[:half], both[half:]).astype(BF16)
            low_y_copy().start()

        @pl.when(s == PAIR_STEP)
        def _():
            low_y_copy().wait_recv()
            lowz[z] = (lowy[0].astype(F32) + lowy[1].astype(F32)).astype(BF16)

            @pl.loop(1, N_Z)
            def _(k):
                low_z_copy(z, lax.rem(z + k, N_Z)).start()

            @pl.loop(0, tensor)
            def _(k):
                x_copy(ball, bx_s, bx_r, k, 1 - g).wait_recv()

            dp_copy(ball, 1, d).start()

        @pl.when(s == SUM_STEP)
        def _():
            @pl.loop(1, N_Z)
            def _(k):
                low_z_copy(lax.rem(z + k, N_Z), z).wait_recv()

            total = lowz[0].astype(F32)
            for k in range(1, N_Z):
                total = total + lowz[k].astype(F32)
            total = total.astype(BF16).astype(F32)
            other = pltpu.roll(total, rank, 1)
            low_lane = lanes(total.shape) < rank
            upper = jnp.where(low_lane, total, other)
            lower = jnp.where(low_lane, other, total)
            for k in range(2 * tensor // 2):
                for n, values in enumerate((upper, lower)):
                    span = pl.ds(n * half, half)
                    wanted = pos[span, :] == 2 * k + lanes(values.shape) // rank
                    wid[span, pl.ds(k * pair, pair)] = jnp.where(wanted, values, 0.0).astype(BF16)
            dp_copy(ball, 1, 1 - d).wait_recv()

        mr = s - Y_LAG - HOP_LAG * z

        @pl.when((mr >= 0) & (mr < MESSAGES))
        def _():
            @pl.when(z_of(mr) > z)
            def _():
                y_copy(mr).wait_recv()

                @pl.when(z == 0)
                def _():
                    part[1, mr] = (part[1, mr].astype(F32) + yrecv[mr].astype(F32)).astype(BF16)

                @pl.when(z > 0)
                def _():
                    right_copy(mr).wait_recv()
                    part[1, mr] = (
                        part[1, mr].astype(F32) + yrecv[mr].astype(F32) + zl[mr].astype(F32)
                    ).astype(BF16)

                right_copy(mr).start()

        ml = s - Y_LAG - HOP_LAG * (N_Z - 1 - z)

        @pl.when((ml >= 0) & (ml < MESSAGES))
        def _():
            @pl.when(z_of(ml) < z)
            def _():
                y_copy(ml).wait_recv()

                @pl.when(z == N_Z - 1)
                def _():
                    part[1, ml] = (part[1, ml].astype(F32) + yrecv[ml].astype(F32)).astype(BF16)

                @pl.when(z < N_Z - 1)
                def _():
                    left_copy(ml).wait_recv()
                    part[1, ml] = (
                        part[1, ml].astype(F32) + yrecv[ml].astype(F32) + zr[ml].astype(F32)
                    ).astype(BF16)

                left_copy(ml).start()

        mf = s - FINAL_LAG

        @pl.when((mf >= 0) & (mf < MESSAGES))
        def _():
            @pl.when(z_of(mf) == z)
            def _():
                y_copy(mf).wait_recv()
                span, cols = place(mf)
                maps = ball[:, :, cols].reshape(2 * tensor * rank, width)
                total = jnp.dot(wid[span, :], maps, preferred_element_type=F32)
                total = total + part[1, mf].astype(F32) + yrecv[mf].astype(F32)

                @pl.when(z == 0)
                def _():
                    left_copy(mf).wait_recv()
                    out[span, cols] = (total + zr[mf].astype(F32)).astype(BF16)

                @pl.when(z == N_Z - 1)
                def _():
                    right_copy(mf).wait_recv()
                    out[span, cols] = (total + zl[mf].astype(F32)).astype(BF16)

                @pl.when((z > 0) & (z < N_Z - 1))
                def _():
                    left_copy(mf).wait_recv()
                    right_copy(mf).wait_recv()
                    out[span, cols] = (total + zl[mf].astype(F32) + zr[mf].astype(F32)).astype(BF16)

    @pl.loop(0, MESSAGES)
    def _(m):
        y_copy(m).wait_send()

        @pl.when(z_of(m) != z)
        def _():
            right_copy(m).wait_send()

    @pl.loop(1, tensor)
    def _(k):
        a_copy(t, peer(k)).wait_send()
        b_copy(t, peer(k)).wait_send()

    @pl.loop(0, tensor)
    def _(k):
        x_copy(aall, ax_s, ax_r, k, g).wait_send()
        x_copy(ball, bx_s, bx_r, k, g).wait_send()

    @pl.loop(1, N_Z)
    def _(k):
        low_z_copy(z, lax.rem(z + k, N_Z)).wait_send()

    low_y_copy().wait_send()
    dp_copy(aall, 0, d).wait_send()
    dp_copy(ball, 1, d).wait_send()


def local_fused(gate, up, w, a, b, row_adapter_index, adapter_storage_slot):
    adapters = adapter_storage_slot.shape[0]
    compare = row_adapter_index[:, None] == jnp.arange(adapters, dtype=jnp.int32)[None, :]
    slot = jnp.sum(jnp.where(compare, adapter_storage_slot[None, :], 0), axis=1)
    tensor = N_Y * N_Z
    rows, depth = gate.shape
    rank = a.shape[1]
    block_cols = w.shape[1] // tensor
    width = block_cols // CHUNKS
    pos = jnp.broadcast_to(slot[:, None], (rows, 2 * rank))
    stage_rows = 64
    hbm = pl.BlockSpec(memory_space=pl.ANY)
    vmem = pl.BlockSpec(memory_space=pltpu.VMEM)
    dma = pltpu.SemaphoreType.DMA
    return pl.pallas_call(
        fused,
        out_shape=jax.ShapeDtypeStruct((rows, block_cols), BF16),
        in_specs=[hbm] * 5 + [vmem],
        out_specs=vmem,
        scratch_shapes=[
            pltpu.VMEM((rows, depth), BF16),
            pltpu.VMEM((2, MESSAGES, rows // PARTS, width), BF16),
            pltpu.VMEM((MESSAGES, rows // PARTS, width), BF16),
            pltpu.VMEM((MESSAGES, rows // PARTS, width), BF16),
            pltpu.VMEM((MESSAGES, rows // PARTS, width), BF16),
            pltpu.VMEM((W_SLOTS, depth, width), BF16),
            pltpu.VMEM((2, 2, stage_rows, depth), BF16),
            pltpu.VMEM((adapters, rank, depth), BF16),
            pltpu.VMEM((adapters, rank, block_cols), BF16),
            pltpu.VMEM((2, rows // 2, 2 * rank), BF16),
            pltpu.VMEM((N_Z, rows // 2, 2 * rank), BF16),
            pltpu.VMEM((rows, adapters * rank), BF16),
            dma((MESSAGES,)), dma((MESSAGES,)), dma((MESSAGES,)), dma((MESSAGES,)), dma((MESSAGES,)),
            dma((W_SLOTS,)), dma((2, 2)),
            dma((tensor,)), dma((tensor,)), dma((tensor,)), dma((tensor,)),
            dma((tensor,)), dma((tensor,)), dma((tensor,)), dma((tensor,)),
            dma((1,)), dma((1,)), dma((N_Z,)), dma((N_Z,)),
            dma((2,)), dma((2,)), dma((2,)),
        ],
        compiler_params=pltpu.CompilerParams(
            collective_id=0, has_side_effects=True, vmem_limit_bytes=60 * 1024 * 1024
        ),
    )(gate, up, w, a, b, pos)


def local(
    gate_preactivation,
    up_preactivation,
    down_matrix,
    adapter_input_maps,
    adapter_output_maps,
    row_adapter_index,
    adapter_storage_slot,
):
    hidden = (
        jax.nn.silu(gate_preactivation.astype(jnp.float32)) * up_preactivation.astype(jnp.float32)
    ).astype(jnp.bfloat16)
    tensor_count = lax.axis_size("tensor")
    data_count = lax.axis_size("dp")
    adapter_count = adapter_storage_slot.shape[0]
    compare = row_adapter_index[:, None] == jnp.arange(adapter_count, dtype=jnp.int32)[None, :]
    slot = jnp.sum(jnp.where(compare, adapter_storage_slot[None, :], 0), axis=1)
    pieces_a, pieces_b = (
        lax.all_gather(adapter_input_maps, "dp", axis=0, tiled=True),
        lax.all_gather(adapter_output_maps, "dp", axis=0, tiled=True),
    )
    pieces_a, pieces_b = (
        lax.all_to_all(pieces_a, "tensor", split_axis=2, concat_axis=0, tiled=True),
        lax.all_to_all(pieces_b, "tensor", split_axis=2, concat_axis=0, tiled=True),
    )
    position = slot % tensor_count * data_count + slot // tensor_count
    row_storage_slots = pieces_a.shape[0]
    rank_projection = pieces_a.shape[1]
    onehot = position[:, None] == jnp.arange(row_storage_slots, dtype=jnp.int32)[None, :]
    flattened_input_maps = pieces_a.reshape(row_storage_slots * rank_projection, pieces_a.shape[2])
    inner = lax.dot_general(
        hidden, flattened_input_maps, (((1,), (1,)), ((), ())), preferred_element_type=jnp.float32
    )
    low_part = jnp.sum(
        inner.reshape(-1, row_storage_slots, rank_projection)
        * onehot[:, :, None].astype(jnp.float32),
        axis=1,
    )
    low_b = lax.psum(low_part.astype(jnp.bfloat16), "tensor")
    widened_rows = (onehot[:, :, None].astype(jnp.bfloat16) * low_b[:, None, :]).reshape(
        -1, row_storage_slots * rank_projection
    )
    adapter_output = jnp.dot(
        widened_rows,
        pieces_b.reshape(row_storage_slots * rank_projection, pieces_b.shape[2]),
        preferred_element_type=jnp.float32,
    )
    partial_out = jnp.dot(hidden, down_matrix, preferred_element_type=jnp.float32)
    base = lax.psum_scatter(
        partial_out.astype(jnp.bfloat16), "tensor", scatter_dimension=1, tiled=True
    ).astype(jnp.float32)
    return (base + adapter_output).astype(jnp.bfloat16)


def solution(mesh):
    placed = (
        P(("groups", "dp"), "tensor"),
        P(("groups", "dp"), "tensor"),
        P("tensor", None),
        P(("dp", "tensor"), None, None),
        P(("dp", "tensor"), None, None),
        P(("groups", "dp")),
        P(),
    )
    sizes = dict(mesh.shape)
    fits = sizes["tensor"] == N_Y * N_Z and sizes["dp"] == 2 and sizes["groups"] == 2
    return jax.shard_map(
        local_fused if fits else local, mesh=mesh, in_specs=placed, out_specs=P(("groups", "dp"), "tensor"), check_vma=False
    )
```

```python
import functools

import jax
import jax.numpy as jnp
from jax import lax
from jax.experimental import pallas as pl
from jax.experimental.pallas import tpu as pltpu
from jax.sharding import PartitionSpec as P

MESH = pl.DeviceIdType.MESH
F32, BF16 = jnp.float32, jnp.bfloat16
N_Y, N_Z = 2, 4
CHUNKS = 4
PARTS = 2
MESSAGES = CHUNKS * N_Z * PARTS
W_SLOTS = 4
Y_LAG, HOP_LAG = 3, 2
Z_FIRST = 1
Z_SUM_LAG = Y_LAG + HOP_LAG * (N_Z - 1) + 2
LOW_STEP, PAIR_STEP, SUM_STEP, FINAL_LAG = 18, 21, 24, 25
STEPS = MESSAGES + FINAL_LAG


def fused(
    gate, up, w, a, b, pos, out,
    hid, part, yrecv, zl, zr, zl2, zr2, wbuf, stage, aall, ball, lowy, lowz, wid,
    y_s, y_r, z_s, zl_r, zr_r, z2_s, zl2_r, zr2_r, w_sem, st_sem, a_s, a_r, b_s, b_r, ax_s, ax_r, bx_s, bx_r,
    ly_s, ly_r, lz_s, lz_r, dp_s, dp_r, own_sem,
):
    tensor = N_Y * N_Z
    t = lax.axis_index("tensor")
    d = lax.axis_index("dp")
    g = lax.axis_index("groups")
    z, y = t // N_Y, t % N_Y
    rows, depth = hid.shape
    block_cols = out.shape[1]
    width = block_cols // CHUNKS
    stage_rows = stage.shape[2]
    part_rows = rows // PARTS

    def peer(k):
        return lax.rem(t + k, tensor)

    def z_of(m):
        return lax.rem(3 * lax.rem(m // PARTS, N_Z), N_Z)

    def z_first(m):
        return (m // (N_Z * PARTS) == Z_FIRST) & (lax.rem(m, PARTS) == PARTS - 1)

    def place(m):
        col = pl.multiple_of(m // (N_Z * PARTS) * width, width)
        row = pl.multiple_of(lax.rem(m, PARTS) * part_rows, part_rows)
        return pl.ds(row, part_rows), pl.ds(col, width)

    rank = aall.shape[1]
    mine = pl.ds(pl.multiple_of(g * (rank // 2), rank // 2), rank // 2)

    def w_copy(j):
        m, own = j // 2 * PARTS, lax.rem(j, 2)
        y_dest = jnp.where(own == 1, y, 1 - y)
        col = (z_of(m) * N_Y + y_dest) * block_cols + m // (N_Z * PARTS) * width
        slot = lax.rem(j, W_SLOTS)
        return pltpu.make_async_copy(
            w.at[:, pl.ds(pl.multiple_of(col, width), width)], wbuf.at[slot], w_sem.at[slot]
        )

    def stage_copies(i):
        s = lax.rem(i, 2)
        span = pl.ds(pl.multiple_of(i * stage_rows, stage_rows), stage_rows)
        return [
            pltpu.make_async_copy(src.at[span, :], stage.at[n, s], st_sem.at[n, s])
            for n, src in enumerate((gate, up))
        ]

    def a_copy(source, dest):
        return pltpu.make_async_remote_copy(
            src_ref=a.at[0, mine, pl.ds(pl.multiple_of(dest * depth, depth), depth)],
            dst_ref=aall.at[d * tensor + source, mine],
            send_sem=a_s.at[dest], recv_sem=a_r.at[source],
            device_id={"tensor": dest}, device_id_type=MESH,
        )

    def b_copy(source, dest):
        return pltpu.make_async_remote_copy(
            src_ref=b.at[0, mine, pl.ds(pl.multiple_of(dest * block_cols, block_cols), block_cols)],
            dst_ref=ball.at[d * tensor + source, mine],
            send_sem=b_s.at[dest], recv_sem=b_r.at[source],
            device_id={"tensor": dest}, device_id_type=MESH,
        )

    def x_copy(buf, send, recv, source, half):
        span = pl.ds(pl.multiple_of(half * (rank // 2), rank // 2), rank // 2)
        return pltpu.make_async_remote_copy(
            src_ref=buf.at[d * tensor + source, span], dst_ref=buf.at[d * tensor + source, span],
            send_sem=send.at[source], recv_sem=recv.at[source],
            device_id={"groups": 1 - g}, device_id_type=MESH,
        )

    def low_y_copy():
        return pltpu.make_async_remote_copy(
            src_ref=lowy.at[0], dst_ref=lowy.at[1], send_sem=ly_s.at[0], recv_sem=ly_r.at[0],
            device_id={"tensor": z * N_Y + 1 - y}, device_id_type=MESH,
        )

    def low_z_copy(source, dest):
        return pltpu.make_async_remote_copy(
            src_ref=lowz.at[source], dst_ref=lowz.at[source],
            send_sem=lz_s.at[dest], recv_sem=lz_r.at[source],
            device_id={"tensor": dest * N_Y + y}, device_id_type=MESH,
        )

    def dp_copy(buf, n, half):
        span = pl.ds(half * tensor, tensor)
        return pltpu.make_async_remote_copy(
            src_ref=buf.at[span], dst_ref=buf.at[span],
            send_sem=dp_s.at[n], recv_sem=dp_r.at[n],
            device_id={"dp": 1 - d}, device_id_type=MESH,
        )

    def y_copy(m):
        return pltpu.make_async_remote_copy(
            src_ref=part.at[0, m], dst_ref=yrecv.at[m],
            send_sem=y_s.at[m], recv_sem=y_r.at[m],
            device_id={"tensor": z * N_Y + 1 - y}, device_id_type=MESH,
        )

    def right_copy(m):
        return pltpu.make_async_remote_copy(
            src_ref=part.at[1, m], dst_ref=zl.at[m],
            send_sem=z_s.at[m], recv_sem=zl_r.at[m],
            device_id={"tensor": lax.rem(t + N_Y, tensor)}, device_id_type=MESH,
        )

    def left_copy(m):
        return pltpu.make_async_remote_copy(
            src_ref=part.at[1, m], dst_ref=zr.at[m],
            send_sem=z_s.at[m], recv_sem=zr_r.at[m],
            device_id={"tensor": lax.rem(t + tensor - N_Y, tensor)}, device_id_type=MESH,
        )

    def right_other(m):
        n = lax.rem(m // PARTS, N_Z)
        return pltpu.make_async_remote_copy(
            src_ref=part.at[0, m], dst_ref=zl2.at[n],
            send_sem=z2_s.at[n], recv_sem=zl2_r.at[n],
            device_id={"tensor": lax.rem(t + N_Y, tensor)}, device_id_type=MESH,
        )

    def left_other(m):
        n = lax.rem(m // PARTS, N_Z)
        return pltpu.make_async_remote_copy(
            src_ref=part.at[0, m], dst_ref=zr2.at[n],
            send_sem=z2_s.at[n], recv_sem=zr2_r.at[n],
            device_id={"tensor": lax.rem(t + tensor - N_Y, tensor)}, device_id_type=MESH,
        )

    def add_to(own, m, buf, n):
        part[own, m] = (part[own, m].astype(F32) + buf[n].astype(F32)).astype(BF16)

    for copy in stage_copies(0):
        copy.start()

    @pl.loop(0, W_SLOTS)
    def _(j):
        w_copy(j).start()

    own_a = pltpu.make_async_copy(
        a.at[0, mine, pl.ds(pl.multiple_of(t * depth, depth), depth)],
        aall.at[d * tensor + t, mine], own_sem.at[0],
    )
    own_b = pltpu.make_async_copy(
        b.at[0, mine, pl.ds(pl.multiple_of(t * block_cols, block_cols), block_cols)],
        ball.at[d * tensor + t, mine], own_sem.at[1],
    )
    own_a.start()
    own_b.start()

    barrier = pltpu.get_barrier_semaphore()

    @pl.loop(1, tensor)
    def _(k):
        pl.semaphore_signal(barrier, inc=1, device_id={"tensor": peer(k)}, device_id_type=MESH)

    pl.semaphore_signal(barrier, inc=1, device_id={"dp": 1 - d}, device_id_type=MESH)
    pl.semaphore_signal(barrier, inc=1, device_id={"groups": 1 - g}, device_id_type=MESH)
    pl.semaphore_wait(barrier, tensor + 1)

    @pl.loop(1, tensor)
    def _(k):
        a_copy(t, peer(k)).start()

    @pl.loop(1, tensor)
    def _(k):
        b_copy(t, peer(k)).start()

    @pl.loop(0, rows // stage_rows)
    def _(i):
        @pl.when(i + 1 < rows // stage_rows)
        def _():
            for copy in stage_copies(i + 1):
                copy.start()

        for copy in stage_copies(i):
            copy.wait()
        s = lax.rem(i, 2)
        v = stage[0, s].astype(F32)
        u = stage[1, s].astype(F32)
        span = pl.ds(pl.multiple_of(i * stage_rows, stage_rows), stage_rows)
        hid[span, :] = (v / (1.0 + jnp.exp(-v)) * u).astype(BF16)

    def lanes(shape):
        return lax.broadcasted_iota(jnp.int32, shape, 1)

    four = 4 * aall.shape[1]
    pair = 2 * aall.shape[1]

    def low_of(first, acc):
        def body(q, acc):
            maps = aall[pl.ds(first + 4 * q, 4)].reshape(four, depth)
            inner = lax.dot_general(hid[...], maps, (((1,), (1,)), ((), ())), preferred_element_type=F32)
            wanted = jnp.concatenate([pos[...]] * 2, axis=1) == first + 4 * q + lanes(inner.shape) // rank
            inner = jnp.where(wanted, inner, 0.0)
            return acc + inner[:, :pair] + inner[:, pair:]

        return lax.fori_loop(0, tensor // 4, body, acc)

    half = rows // 2

    @pl.loop(0, STEPS)
    def _(s):
        @pl.when((s < MESSAGES) & (lax.rem(s, PARTS) == 0))
        def _():
            @pl.loop(0, 2)
            def _(own):
                j = s // PARTS * 2 + own
                w_copy(j).wait()
                prod = jnp.dot(hid[...], wbuf[lax.rem(j, W_SLOTS)], preferred_element_type=F32)
                part[own, pl.ds(s, PARTS)] = prod.astype(BF16).reshape(PARTS, part_rows, width)

                @pl.when(j + W_SLOTS < 2 * MESSAGES // PARTS)
                def _():
                    w_copy(j + W_SLOTS).start()

                @pl.when(own == 0)
                def _():
                    for n in range(PARTS):
                        @pl.when(jnp.logical_not(z_first(s + n)))
                        def _():
                            y_copy(s + n).start()

        @pl.when(s == 0)
        def _():
            own_a.wait()
            x_copy(aall, ax_s, ax_r, t, g).start()

        @pl.when((s >= 6) & (s < 6 + tensor - 1))
        def _():
            source = peer(s - 5)
            a_copy(source, t).wait_recv()
            x_copy(aall, ax_s, ax_r, source, g).start()

        @pl.when(s == LOW_STEP)
        def _():
            own_b.wait()
            x_copy(ball, bx_s, bx_r, t, g).start()

            @pl.loop(1, tensor)
            def _(k):
                b_copy(peer(k), t).wait_recv()
                x_copy(ball, bx_s, bx_r, peer(k), g).start()

            @pl.loop(0, tensor)
            def _(k):
                x_copy(aall, ax_s, ax_r, k, 1 - g).wait_recv()

            dp_copy(aall, 0, d).start()
            acc = low_of(d * tensor, jnp.zeros((rows, pair), F32))
            dp_copy(aall, 0, 1 - d).wait_recv()
            acc = low_of((1 - d) * tensor, acc)
            both = acc + pltpu.roll(acc, rank, 1)
            lowy[0] = jnp.where(lanes((half, pair)) < rank, both[:half], both[half:]).astype(BF16)
            low_y_copy().start()

        @pl.when(s == PAIR_STEP)
        def _():
            low_y_copy().wait_recv()
            lowz[z] = (lowy[0].astype(F32) + lowy[1].astype(F32)).astype(BF16)

            @pl.loop(1, N_Z)
            def _(k):
                low_z_copy(z, lax.rem(z + k, N_Z)).start()

            @pl.loop(0, tensor)
            def _(k):
                x_copy(ball, bx_s, bx_r, k, 1 - g).wait_recv()

            dp_copy(ball, 1, d).start()

        @pl.when(s == SUM_STEP)
        def _():
            @pl.loop(1, N_Z)
            def _(k):
                low_z_copy(lax.rem(z + k, N_Z), z).wait_recv()

            total = lowz[0].astype(F32)
            for k in range(1, N_Z):
                total = total + lowz[k].astype(F32)
            total = total.astype(BF16).astype(F32)
            other = pltpu.roll(total, rank, 1)
            low_lane = lanes(total.shape) < rank
            upper = jnp.where(low_lane, total, other)
            lower = jnp.where(low_lane, other, total)
            for k in range(2 * tensor // 2):
                for n, values in enumerate((upper, lower)):
                    span = pl.ds(n * half, half)
                    wanted = pos[span, :] == 2 * k + lanes(values.shape) // rank
                    wid[span, pl.ds(k * pair, pair)] = jnp.where(wanted, values, 0.0).astype(BF16)
            dp_copy(ball, 1, 1 - d).wait_recv()

        mr = s - Y_LAG - HOP_LAG * z

        @pl.when((mr >= 0) & (mr < MESSAGES))
        def _():
            @pl.when(z_of(mr) > z)
            def _():
                early = z_first(mr)

                @pl.when(early)
                def _():
                    @pl.when(z > 0)
                    def _():
                        right_copy(mr).wait_recv()
                        add_to(1, mr, zl, mr)
                        right_other(mr).wait_recv()
                        add_to(0, mr, zl2, lax.rem(mr // PARTS, N_Z))

                    right_other(mr).start()

                @pl.when(jnp.logical_not(early))
                def _():
                    y_copy(mr).wait_recv()

                    @pl.when(z == 0)
                    def _():
                        add_to(1, mr, yrecv, mr)

                    @pl.when(z > 0)
                    def _():
                        right_copy(mr).wait_recv()
                        part[1, mr] = (
                            part[1, mr].astype(F32) + yrecv[mr].astype(F32) + zl[mr].astype(F32)
                        ).astype(BF16)

                right_copy(mr).start()

        ml = s - Y_LAG - HOP_LAG * (N_Z - 1 - z)

        @pl.when((ml >= 0) & (ml < MESSAGES))
        def _():
            @pl.when(z_of(ml) < z)
            def _():
                early = z_first(ml)

                @pl.when(early)
                def _():
                    @pl.when(z < N_Z - 1)
                    def _():
                        left_copy(ml).wait_recv()
                        add_to(1, ml, zr, ml)
                        left_other(ml).wait_recv()
                        add_to(0, ml, zr2, lax.rem(ml // PARTS, N_Z))

                    left_other(ml).start()

                @pl.when(jnp.logical_not(early))
                def _():
                    y_copy(ml).wait_recv()

                    @pl.when(z == N_Z - 1)
                    def _():
                        add_to(1, ml, yrecv, ml)

                    @pl.when(z < N_Z - 1)
                    def _():
                        left_copy(ml).wait_recv()
                        part[1, ml] = (
                            part[1, ml].astype(F32) + yrecv[ml].astype(F32) + zr[ml].astype(F32)
                        ).astype(BF16)

                left_copy(ml).start()

        mz = s - Z_SUM_LAG

        @pl.when((mz >= 0) & (mz < MESSAGES))
        def _():
            @pl.when(z_first(mz) & (z_of(mz) == z))
            def _():
                n = lax.rem(mz // PARTS, N_Z)

                @pl.when(z == 0)
                def _():
                    left_other(mz).wait_recv()
                    add_to(0, mz, zr2, n)

                @pl.when(z == N_Z - 1)
                def _():
                    right_other(mz).wait_recv()
                    add_to(0, mz, zl2, n)

                @pl.when((z > 0) & (z < N_Z - 1))
                def _():
                    left_other(mz).wait_recv()
                    right_other(mz).wait_recv()
                    part[0, mz] = (
                        part[0, mz].astype(F32) + zl2[n].astype(F32) + zr2[n].astype(F32)
                    ).astype(BF16)

                y_copy(mz).start()

        mf = s - FINAL_LAG

        @pl.when((mf >= 0) & (mf < MESSAGES))
        def _():
            @pl.when(z_of(mf) == z)
            def _():
                y_copy(mf).wait_recv()
                span, cols = place(mf)
                maps = ball[:, :, cols].reshape(2 * tensor * rank, width)
                total = jnp.dot(wid[span, :], maps, preferred_element_type=F32)
                total = total + part[1, mf].astype(F32) + yrecv[mf].astype(F32)

                @pl.when(z == 0)
                def _():
                    left_copy(mf).wait_recv()
                    out[span, cols] = (total + zr[mf].astype(F32)).astype(BF16)

                @pl.when(z == N_Z - 1)
                def _():
                    right_copy(mf).wait_recv()
                    out[span, cols] = (total + zl[mf].astype(F32)).astype(BF16)

                @pl.when((z > 0) & (z < N_Z - 1))
                def _():
                    left_copy(mf).wait_recv()
                    right_copy(mf).wait_recv()
                    out[span, cols] = (total + zl[mf].astype(F32) + zr[mf].astype(F32)).astype(BF16)

    @pl.loop(0, MESSAGES)
    def _(m):
        early = z_first(m)

        @pl.when(jnp.logical_not(early) | (z_of(m) == z))
        def _():
            y_copy(m).wait_send()

        @pl.when(z_of(m) != z)
        def _():
            right_copy(m).wait_send()

            @pl.when(early)
            def _():
                right_other(m).wait_send()

    @pl.loop(1, tensor)
    def _(k):
        a_copy(t, peer(k)).wait_send()
        b_copy(t, peer(k)).wait_send()

    @pl.loop(0, tensor)
    def _(k):
        x_copy(aall, ax_s, ax_r, k, g).wait_send()
        x_copy(ball, bx_s, bx_r, k, g).wait_send()

    @pl.loop(1, N_Z)
    def _(k):
        low_z_copy(z, lax.rem(z + k, N_Z)).wait_send()

    low_y_copy().wait_send()
    dp_copy(aall, 0, d).wait_send()
    dp_copy(ball, 1, d).wait_send()


def local_fused(gate, up, w, a, b, row_adapter_index, adapter_storage_slot):
    adapters = adapter_storage_slot.shape[0]
    compare = row_adapter_index[:, None] == jnp.arange(adapters, dtype=jnp.int32)[None, :]
    slot = jnp.sum(jnp.where(compare, adapter_storage_slot[None, :], 0), axis=1)
    tensor = N_Y * N_Z
    rows, depth = gate.shape
    rank = a.shape[1]
    block_cols = w.shape[1] // tensor
    width = block_cols // CHUNKS
    pos = jnp.broadcast_to(slot[:, None], (rows, 2 * rank))
    stage_rows = 64
    hbm = pl.BlockSpec(memory_space=pl.ANY)
    vmem = pl.BlockSpec(memory_space=pltpu.VMEM)
    dma = pltpu.SemaphoreType.DMA
    return pl.pallas_call(
        fused,
        out_shape=jax.ShapeDtypeStruct((rows, block_cols), BF16),
        in_specs=[hbm] * 5 + [vmem],
        out_specs=vmem,
        scratch_shapes=[
            pltpu.VMEM((rows, depth), BF16),
            pltpu.VMEM((2, MESSAGES, rows // PARTS, width), BF16),
            pltpu.VMEM((MESSAGES, rows // PARTS, width), BF16),
            pltpu.VMEM((MESSAGES, rows // PARTS, width), BF16),
            pltpu.VMEM((MESSAGES, rows // PARTS, width), BF16),
            pltpu.VMEM((N_Z, rows // PARTS, width), BF16),
            pltpu.VMEM((N_Z, rows // PARTS, width), BF16),
            pltpu.VMEM((W_SLOTS, depth, width), BF16),
            pltpu.VMEM((2, 2, stage_rows, depth), BF16),
            pltpu.VMEM((adapters, rank, depth), BF16),
            pltpu.VMEM((adapters, rank, block_cols), BF16),
            pltpu.VMEM((2, rows // 2, 2 * rank), BF16),
            pltpu.VMEM((N_Z, rows // 2, 2 * rank), BF16),
            pltpu.VMEM((rows, adapters * rank), BF16),
            dma((MESSAGES,)), dma((MESSAGES,)), dma((MESSAGES,)), dma((MESSAGES,)), dma((MESSAGES,)),
            dma((N_Z,)), dma((N_Z,)), dma((N_Z,)),
            dma((W_SLOTS,)), dma((2, 2)),
            dma((tensor,)), dma((tensor,)), dma((tensor,)), dma((tensor,)),
            dma((tensor,)), dma((tensor,)), dma((tensor,)), dma((tensor,)),
            dma((1,)), dma((1,)), dma((N_Z,)), dma((N_Z,)),
            dma((2,)), dma((2,)), dma((2,)),
        ],
        compiler_params=pltpu.CompilerParams(
            collective_id=0, has_side_effects=True, vmem_limit_bytes=60 * 1024 * 1024
        ),
    )(gate, up, w, a, b, pos)


def local(
    gate_preactivation,
    up_preactivation,
    down_matrix,
    adapter_input_maps,
    adapter_output_maps,
    row_adapter_index,
    adapter_storage_slot,
):
    hidden = (
        jax.nn.silu(gate_preactivation.astype(jnp.float32)) * up_preactivation.astype(jnp.float32)
    ).astype(jnp.bfloat16)
    tensor_count = lax.axis_size("tensor")
    data_count = lax.axis_size("dp")
    adapter_count = adapter_storage_slot.shape[0]
    compare = row_adapter_index[:, None] == jnp.arange(adapter_count, dtype=jnp.int32)[None, :]
    slot = jnp.sum(jnp.where(compare, adapter_storage_slot[None, :], 0), axis=1)
    pieces_a, pieces_b = (
        lax.all_gather(adapter_input_maps, "dp", axis=0, tiled=True),
        lax.all_gather(adapter_output_maps, "dp", axis=0, tiled=True),
    )
    pieces_a, pieces_b = (
        lax.all_to_all(pieces_a, "tensor", split_axis=2, concat_axis=0, tiled=True),
        lax.all_to_all(pieces_b, "tensor", split_axis=2, concat_axis=0, tiled=True),
    )
    position = slot % tensor_count * data_count + slot // tensor_count
    row_storage_slots = pieces_a.shape[0]
    rank_projection = pieces_a.shape[1]
    onehot = position[:, None] == jnp.arange(row_storage_slots, dtype=jnp.int32)[None, :]
    flattened_input_maps = pieces_a.reshape(row_storage_slots * rank_projection, pieces_a.shape[2])
    inner = lax.dot_general(
        hidden, flattened_input_maps, (((1,), (1,)), ((), ())), preferred_element_type=jnp.float32
    )
    low_part = jnp.sum(
        inner.reshape(-1, row_storage_slots, rank_projection)
        * onehot[:, :, None].astype(jnp.float32),
        axis=1,
    )
    low_b = lax.psum(low_part.astype(jnp.bfloat16), "tensor")
    widened_rows = (onehot[:, :, None].astype(jnp.bfloat16) * low_b[:, None, :]).reshape(
        -1, row_storage_slots * rank_projection
    )
    adapter_output = jnp.dot(
        widened_rows,
        pieces_b.reshape(row_storage_slots * rank_projection, pieces_b.shape[2]),
        preferred_element_type=jnp.float32,
    )
    partial_out = jnp.dot(hidden, down_matrix, preferred_element_type=jnp.float32)
    base = lax.psum_scatter(
        partial_out.astype(jnp.bfloat16), "tensor", scatter_dimension=1, tiled=True
    ).astype(jnp.float32)
    return (base + adapter_output).astype(jnp.bfloat16)


def solution(mesh):
    placed = (
        P(("groups", "dp"), "tensor"),
        P(("groups", "dp"), "tensor"),
        P("tensor", None),
        P(("dp", "tensor"), None, None),
        P(("dp", "tensor"), None, None),
        P(("groups", "dp")),
        P(),
    )
    sizes = dict(mesh.shape)
    fits = sizes["tensor"] == N_Y * N_Z and sizes["dp"] == 2 and sizes["groups"] == 2
    return jax.shard_map(
        local_fused if fits else local, mesh=mesh, in_specs=placed, out_specs=P(("groups", "dp"), "tensor"), check_vma=False
    )
```

```python
import functools

import jax
import jax.numpy as jnp
from jax import lax
from jax.experimental import pallas as pl
from jax.experimental.pallas import tpu as pltpu
from jax.sharding import PartitionSpec as P

MESH = pl.DeviceIdType.MESH
F32, BF16 = jnp.float32, jnp.bfloat16
N_Y, N_Z = 2, 4
CHUNKS = 4
PARTS = 3
MESSAGES = CHUNKS * N_Z * PARTS
W_SLOTS = 4
Y_LAG, HOP_LAG = 6, 3
Z_FIRST = 1
Z_SUM_LAG = Y_LAG + HOP_LAG * (N_Z - 1) + 2
LOW_STEP, PAIR_STEP, SUM_STEP, FINAL_LAG = 27, 31, 36, 37
STEPS = MESSAGES + FINAL_LAG


def fused(
    gate, up, w, a, b, pos, out,
    hid, part, yrecv, zl, zr, zl2, zr2, wbuf, stage, aall, ball, lowy, lowz, wid,
    y_s, y_r, z_s, zl_r, zr_r, z2_s, zl2_r, zr2_r, w_sem, st_sem, a_s, a_r, b_s, b_r, ax_s, ax_r, bx_s, bx_r,
    ly_s, ly_r, lz_s, lz_r, dp_s, dp_r, own_sem,
):
    tensor = N_Y * N_Z
    t = lax.axis_index("tensor")
    d = lax.axis_index("dp")
    g = lax.axis_index("groups")
    z, y = t // N_Y, t % N_Y
    rows, depth = hid.shape
    block_cols = out.shape[1]
    width = block_cols // CHUNKS
    stage_rows = stage.shape[2]
    part_rows = rows // PARTS

    def peer(k):
        return lax.rem(t + k, tensor)

    def z_of(m):
        return lax.rem(3 * lax.rem(m // PARTS, N_Z), N_Z)

    def z_first(m):
        return (m // (N_Z * PARTS) == Z_FIRST) & (lax.rem(m, PARTS) == PARTS - 1)

    def place(m):
        col = pl.multiple_of(m // (N_Z * PARTS) * width, width)
        row = pl.multiple_of(lax.rem(m, PARTS) * part_rows, part_rows)
        return pl.ds(row, part_rows), pl.ds(col, width)

    rank = aall.shape[1]
    mine = pl.ds(pl.multiple_of(g * (rank // 2), rank // 2), rank // 2)

    def w_copy(j):
        m, own = j // 2 * PARTS, lax.rem(j, 2)
        y_dest = jnp.where(own == 1, y, 1 - y)
        col = (z_of(m) * N_Y + y_dest) * block_cols + m // (N_Z * PARTS) * width
        slot = lax.rem(j, W_SLOTS)
        return pltpu.make_async_copy(
            w.at[:, pl.ds(pl.multiple_of(col, width), width)], wbuf.at[slot], w_sem.at[slot]
        )

    def stage_copies(i):
        s = lax.rem(i, 2)
        span = pl.ds(pl.multiple_of(i * stage_rows, stage_rows), stage_rows)
        return [
            pltpu.make_async_copy(src.at[span, :], stage.at[n, s], st_sem.at[n, s])
            for n, src in enumerate((gate, up))
        ]

    def a_copy(source, dest):
        return pltpu.make_async_remote_copy(
            src_ref=a.at[0, mine, pl.ds(pl.multiple_of(dest * depth, depth), depth)],
            dst_ref=aall.at[d * tensor + source, mine],
            send_sem=a_s.at[dest], recv_sem=a_r.at[source],
            device_id={"tensor": dest}, device_id_type=MESH,
        )

    def b_copy(source, dest):
        return pltpu.make_async_remote_copy(
            src_ref=b.at[0, mine, pl.ds(pl.multiple_of(dest * block_cols, block_cols), block_cols)],
            dst_ref=ball.at[d * tensor + source, mine],
            send_sem=b_s.at[dest], recv_sem=b_r.at[source],
            device_id={"tensor": dest}, device_id_type=MESH,
        )

    def x_copy(buf, send, recv, source, half):
        span = pl.ds(pl.multiple_of(half * (rank // 2), rank // 2), rank // 2)
        return pltpu.make_async_remote_copy(
            src_ref=buf.at[d * tensor + source, span], dst_ref=buf.at[d * tensor + source, span],
            send_sem=send.at[source], recv_sem=recv.at[source],
            device_id={"groups": 1 - g}, device_id_type=MESH,
        )

    def low_y_copy():
        return pltpu.make_async_remote_copy(
            src_ref=lowy.at[0], dst_ref=lowy.at[1], send_sem=ly_s.at[0], recv_sem=ly_r.at[0],
            device_id={"tensor": z * N_Y + 1 - y}, device_id_type=MESH,
        )

    def low_z_copy(source, dest):
        return pltpu.make_async_remote_copy(
            src_ref=lowz.at[source], dst_ref=lowz.at[source],
            send_sem=lz_s.at[dest], recv_sem=lz_r.at[source],
            device_id={"tensor": dest * N_Y + y}, device_id_type=MESH,
        )

    def dp_copy(buf, n, half):
        span = pl.ds(half * tensor, tensor)
        return pltpu.make_async_remote_copy(
            src_ref=buf.at[span], dst_ref=buf.at[span],
            send_sem=dp_s.at[n], recv_sem=dp_r.at[n],
            device_id={"dp": 1 - d}, device_id_type=MESH,
        )

    def y_copy(m):
        return pltpu.make_async_remote_copy(
            src_ref=part.at[0, m], dst_ref=yrecv.at[m],
            send_sem=y_s.at[m], recv_sem=y_r.at[m],
            device_id={"tensor": z * N_Y + 1 - y}, device_id_type=MESH,
        )

    def right_copy(m):
        return pltpu.make_async_remote_copy(
            src_ref=part.at[1, m], dst_ref=zl.at[m],
            send_sem=z_s.at[m], recv_sem=zl_r.at[m],
            device_id={"tensor": lax.rem(t + N_Y, tensor)}, device_id_type=MESH,
        )

    def left_copy(m):
        return pltpu.make_async_remote_copy(
            src_ref=part.at[1, m], dst_ref=zr.at[m],
            send_sem=z_s.at[m], recv_sem=zr_r.at[m],
            device_id={"tensor": lax.rem(t + tensor - N_Y, tensor)}, device_id_type=MESH,
        )

    def right_other(m):
        n = lax.rem(m // PARTS, N_Z)
        return pltpu.make_async_remote_copy(
            src_ref=part.at[0, m], dst_ref=zl2.at[n],
            send_sem=z2_s.at[n], recv_sem=zl2_r.at[n],
            device_id={"tensor": lax.rem(t + N_Y, tensor)}, device_id_type=MESH,
        )

    def left_other(m):
        n = lax.rem(m // PARTS, N_Z)
        return pltpu.make_async_remote_copy(
            src_ref=part.at[0, m], dst_ref=zr2.at[n],
            send_sem=z2_s.at[n], recv_sem=zr2_r.at[n],
            device_id={"tensor": lax.rem(t + tensor - N_Y, tensor)}, device_id_type=MESH,
        )

    def add_to(own, m, buf, n):
        part[own, m] = (part[own, m].astype(F32) + buf[n].astype(F32)).astype(BF16)

    for copy in stage_copies(0):
        copy.start()

    @pl.loop(0, W_SLOTS)
    def _(j):
        w_copy(j).start()

    own_a = pltpu.make_async_copy(
        a.at[0, mine, pl.ds(pl.multiple_of(t * depth, depth), depth)],
        aall.at[d * tensor + t, mine], own_sem.at[0],
    )
    own_b = pltpu.make_async_copy(
        b.at[0, mine, pl.ds(pl.multiple_of(t * block_cols, block_cols), block_cols)],
        ball.at[d * tensor + t, mine], own_sem.at[1],
    )
    own_a.start()
    own_b.start()

    barrier = pltpu.get_barrier_semaphore()

    @pl.loop(1, tensor)
    def _(k):
        pl.semaphore_signal(barrier, inc=1, device_id={"tensor": peer(k)}, device_id_type=MESH)

    pl.semaphore_signal(barrier, inc=1, device_id={"dp": 1 - d}, device_id_type=MESH)
    pl.semaphore_signal(barrier, inc=1, device_id={"groups": 1 - g}, device_id_type=MESH)
    pl.semaphore_wait(barrier, tensor + 1)

    @pl.loop(1, tensor)
    def _(k):
        a_copy(t, peer(k)).start()

    @pl.loop(1, tensor)
    def _(k):
        b_copy(t, peer(k)).start()

    @pl.loop(0, rows // stage_rows)
    def _(i):
        @pl.when(i + 1 < rows // stage_rows)
        def _():
            for copy in stage_copies(i + 1):
                copy.start()

        for copy in stage_copies(i):
            copy.wait()
        s = lax.rem(i, 2)
        v = stage[0, s].astype(F32)
        u = stage[1, s].astype(F32)
        span = pl.ds(pl.multiple_of(i * stage_rows, stage_rows), stage_rows)
        hid[span, :] = (v / (1.0 + jnp.exp(-v)) * u).astype(BF16)

    def lanes(shape):
        return lax.broadcasted_iota(jnp.int32, shape, 1)

    four = 4 * aall.shape[1]
    pair = 2 * aall.shape[1]

    def low_of(first, acc):
        def body(q, acc):
            maps = aall[pl.ds(first + 4 * q, 4)].reshape(four, depth)
            inner = lax.dot_general(hid[...], maps, (((1,), (1,)), ((), ())), preferred_element_type=F32)
            wanted = jnp.concatenate([pos[...]] * 2, axis=1) == first + 4 * q + lanes(inner.shape) // rank
            inner = jnp.where(wanted, inner, 0.0)
            return acc + inner[:, :pair] + inner[:, pair:]

        return lax.fori_loop(0, tensor // 4, body, acc)

    half = rows // 2

    @pl.loop(0, STEPS)
    def _(s):
        @pl.when((s < MESSAGES) & (lax.rem(s, PARTS) == 0))
        def _():
            @pl.loop(0, 2)
            def _(own):
                j = s // PARTS * 2 + own
                w_copy(j).wait()
                prod = jnp.dot(hid[...], wbuf[lax.rem(j, W_SLOTS)], preferred_element_type=F32)
                part[own, pl.ds(s, PARTS)] = prod.astype(BF16).reshape(PARTS, part_rows, width)

                @pl.when(j + W_SLOTS < 2 * MESSAGES // PARTS)
                def _():
                    w_copy(j + W_SLOTS).start()

                @pl.when(own == 0)
                def _():
                    for n in range(PARTS):
                        @pl.when(jnp.logical_not(z_first(s + n)))
                        def _():
                            y_copy(s + n).start()

        @pl.when(s == 0)
        def _():
            own_a.wait()
            x_copy(aall, ax_s, ax_r, t, g).start()

        @pl.when((s >= 6) & (s < 6 + tensor - 1))
        def _():
            source = peer(s - 5)
            a_copy(source, t).wait_recv()
            x_copy(aall, ax_s, ax_r, source, g).start()

        @pl.when(s == LOW_STEP)
        def _():
            own_b.wait()
            x_copy(ball, bx_s, bx_r, t, g).start()

            @pl.loop(1, tensor)
            def _(k):
                b_copy(peer(k), t).wait_recv()
                x_copy(ball, bx_s, bx_r, peer(k), g).start()

            @pl.loop(0, tensor)
            def _(k):
                x_copy(aall, ax_s, ax_r, k, 1 - g).wait_recv()

            dp_copy(aall, 0, d).start()
            acc = low_of(d * tensor, jnp.zeros((rows, pair), F32))
            dp_copy(aall, 0, 1 - d).wait_recv()
            acc = low_of((1 - d) * tensor, acc)
            both = acc + pltpu.roll(acc, rank, 1)
            lowy[0] = jnp.where(lanes((half, pair)) < rank, both[:half], both[half:]).astype(BF16)
            low_y_copy().start()

        @pl.when(s == PAIR_STEP)
        def _():
            low_y_copy().wait_recv()
            lowz[z] = (lowy[0].astype(F32) + lowy[1].astype(F32)).astype(BF16)

            @pl.loop(1, N_Z)
            def _(k):
                low_z_copy(z, lax.rem(z + k, N_Z)).start()

            @pl.loop(0, tensor)
            def _(k):
                x_copy(ball, bx_s, bx_r, k, 1 - g).wait_recv()

            dp_copy(ball, 1, d).start()

        @pl.when(s == SUM_STEP)
        def _():
            @pl.loop(1, N_Z)
            def _(k):
                low_z_copy(lax.rem(z + k, N_Z), z).wait_recv()

            total = lowz[0].astype(F32)
            for k in range(1, N_Z):
                total = total + lowz[k].astype(F32)
            total = total.astype(BF16).astype(F32)
            other = pltpu.roll(total, rank, 1)
            low_lane = lanes(total.shape) < rank
            upper = jnp.where(low_lane, total, other)
            lower = jnp.where(low_lane, other, total)
            for k in range(2 * tensor // 2):
                for n, values in enumerate((upper, lower)):
                    span = pl.ds(n * half, half)
                    wanted = pos[span, :] == 2 * k + lanes(values.shape) // rank
                    wid[span, pl.ds(k * pair, pair)] = jnp.where(wanted, values, 0.0).astype(BF16)
            dp_copy(ball, 1, 1 - d).wait_recv()

        mr = s - Y_LAG - HOP_LAG * z

        @pl.when((mr >= 0) & (mr < MESSAGES))
        def _():
            @pl.when(z_of(mr) > z)
            def _():
                early = z_first(mr)

                @pl.when(early)
                def _():
                    @pl.when(z > 0)
                    def _():
                        right_copy(mr).wait_recv()
                        add_to(1, mr, zl, mr)
                        right_other(mr).wait_recv()
                        add_to(0, mr, zl2, lax.rem(mr // PARTS, N_Z))

                    right_other(mr).start()

                @pl.when(jnp.logical_not(early))
                def _():
                    y_copy(mr).wait_recv()

                    @pl.when(z == 0)
                    def _():
                        add_to(1, mr, yrecv, mr)

                    @pl.when(z > 0)
                    def _():
                        right_copy(mr).wait_recv()
                        part[1, mr] = (
                            part[1, mr].astype(F32) + yrecv[mr].astype(F32) + zl[mr].astype(F32)
                        ).astype(BF16)

                right_copy(mr).start()

        ml = s - Y_LAG - HOP_LAG * (N_Z - 1 - z)

        @pl.when((ml >= 0) & (ml < MESSAGES))
        def _():
            @pl.when(z_of(ml) < z)
            def _():
                early = z_first(ml)

                @pl.when(early)
                def _():
                    @pl.when(z < N_Z - 1)
                    def _():
                        left_copy(ml).wait_recv()
                        add_to(1, ml, zr, ml)
                        left_other(ml).wait_recv()
                        add_to(0, ml, zr2, lax.rem(ml // PARTS, N_Z))

                    left_other(ml).start()

                @pl.when(jnp.logical_not(early))
                def _():
                    y_copy(ml).wait_recv()

                    @pl.when(z == N_Z - 1)
                    def _():
                        add_to(1, ml, yrecv, ml)

                    @pl.when(z < N_Z - 1)
                    def _():
                        left_copy(ml).wait_recv()
                        part[1, ml] = (
                            part[1, ml].astype(F32) + yrecv[ml].astype(F32) + zr[ml].astype(F32)
                        ).astype(BF16)

                left_copy(ml).start()

        mz = s - Z_SUM_LAG

        @pl.when((mz >= 0) & (mz < MESSAGES))
        def _():
            @pl.when(z_first(mz) & (z_of(mz) == z))
            def _():
                n = lax.rem(mz // PARTS, N_Z)

                @pl.when(z == 0)
                def _():
                    left_other(mz).wait_recv()
                    add_to(0, mz, zr2, n)

                @pl.when(z == N_Z - 1)
                def _():
                    right_other(mz).wait_recv()
                    add_to(0, mz, zl2, n)

                @pl.when((z > 0) & (z < N_Z - 1))
                def _():
                    left_other(mz).wait_recv()
                    right_other(mz).wait_recv()
                    part[0, mz] = (
                        part[0, mz].astype(F32) + zl2[n].astype(F32) + zr2[n].astype(F32)
                    ).astype(BF16)

                y_copy(mz).start()

        mf = s - FINAL_LAG

        @pl.when((mf >= 0) & (mf < MESSAGES))
        def _():
            @pl.when(z_of(mf) == z)
            def _():
                y_copy(mf).wait_recv()
                span, cols = place(mf)
                maps = ball[:, :, cols].reshape(2 * tensor * rank, width)
                total = jnp.dot(wid[span, :], maps, preferred_element_type=F32)
                total = total + part[1, mf].astype(F32) + yrecv[mf].astype(F32)

                @pl.when(z == 0)
                def _():
                    left_copy(mf).wait_recv()
                    out[span, cols] = (total + zr[mf].astype(F32)).astype(BF16)

                @pl.when(z == N_Z - 1)
                def _():
                    right_copy(mf).wait_recv()
                    out[span, cols] = (total + zl[mf].astype(F32)).astype(BF16)

                @pl.when((z > 0) & (z < N_Z - 1))
                def _():
                    left_copy(mf).wait_recv()
                    right_copy(mf).wait_recv()
                    out[span, cols] = (total + zl[mf].astype(F32) + zr[mf].astype(F32)).astype(BF16)

    @pl.loop(0, MESSAGES)
    def _(m):
        early = z_first(m)

        @pl.when(jnp.logical_not(early) | (z_of(m) == z))
        def _():
            y_copy(m).wait_send()

        @pl.when(z_of(m) != z)
        def _():
            right_copy(m).wait_send()

            @pl.when(early)
            def _():
                right_other(m).wait_send()

    @pl.loop(1, tensor)
    def _(k):
        a_copy(t, peer(k)).wait_send()
        b_copy(t, peer(k)).wait_send()

    @pl.loop(0, tensor)
    def _(k):
        x_copy(aall, ax_s, ax_r, k, g).wait_send()
        x_copy(ball, bx_s, bx_r, k, g).wait_send()

    @pl.loop(1, N_Z)
    def _(k):
        low_z_copy(z, lax.rem(z + k, N_Z)).wait_send()

    low_y_copy().wait_send()
    dp_copy(aall, 0, d).wait_send()
    dp_copy(ball, 1, d).wait_send()


def local_fused(gate, up, w, a, b, row_adapter_index, adapter_storage_slot):
    adapters = adapter_storage_slot.shape[0]
    compare = row_adapter_index[:, None] == jnp.arange(adapters, dtype=jnp.int32)[None, :]
    slot = jnp.sum(jnp.where(compare, adapter_storage_slot[None, :], 0), axis=1)
    tensor = N_Y * N_Z
    rows, depth = gate.shape
    rank = a.shape[1]
    block_cols = w.shape[1] // tensor
    width = block_cols // CHUNKS
    pos = jnp.broadcast_to(slot[:, None], (rows, 2 * rank))
    stage_rows = 64
    hbm = pl.BlockSpec(memory_space=pl.ANY)
    vmem = pl.BlockSpec(memory_space=pltpu.VMEM)
    dma = pltpu.SemaphoreType.DMA
    return pl.pallas_call(
        fused,
        out_shape=jax.ShapeDtypeStruct((rows, block_cols), BF16),
        in_specs=[hbm] * 5 + [vmem],
        out_specs=vmem,
        scratch_shapes=[
            pltpu.VMEM((rows, depth), BF16),
            pltpu.VMEM((2, MESSAGES, rows // PARTS, width), BF16),
            pltpu.VMEM((MESSAGES, rows // PARTS, width), BF16),
            pltpu.VMEM((MESSAGES, rows // PARTS, width), BF16),
            pltpu.VMEM((MESSAGES, rows // PARTS, width), BF16),
            pltpu.VMEM((N_Z, rows // PARTS, width), BF16),
            pltpu.VMEM((N_Z, rows // PARTS, width), BF16),
            pltpu.VMEM((W_SLOTS, depth, width), BF16),
            pltpu.VMEM((2, 2, stage_rows, depth), BF16),
            pltpu.VMEM((adapters, rank, depth), BF16),
            pltpu.VMEM((adapters, rank, block_cols), BF16),
            pltpu.VMEM((2, rows // 2, 2 * rank), BF16),
            pltpu.VMEM((N_Z, rows // 2, 2 * rank), BF16),
            pltpu.VMEM((rows, adapters * rank), BF16),
            dma((MESSAGES,)), dma((MESSAGES,)), dma((MESSAGES,)), dma((MESSAGES,)), dma((MESSAGES,)),
            dma((N_Z,)), dma((N_Z,)), dma((N_Z,)),
            dma((W_SLOTS,)), dma((2, 2)),
            dma((tensor,)), dma((tensor,)), dma((tensor,)), dma((tensor,)),
            dma((tensor,)), dma((tensor,)), dma((tensor,)), dma((tensor,)),
            dma((1,)), dma((1,)), dma((N_Z,)), dma((N_Z,)),
            dma((2,)), dma((2,)), dma((2,)),
        ],
        compiler_params=pltpu.CompilerParams(
            collective_id=0, has_side_effects=True, vmem_limit_bytes=60 * 1024 * 1024
        ),
    )(gate, up, w, a, b, pos)


def local(
    gate_preactivation,
    up_preactivation,
    down_matrix,
    adapter_input_maps,
    adapter_output_maps,
    row_adapter_index,
    adapter_storage_slot,
):
    hidden = (
        jax.nn.silu(gate_preactivation.astype(jnp.float32)) * up_preactivation.astype(jnp.float32)
    ).astype(jnp.bfloat16)
    tensor_count = lax.axis_size("tensor")
    data_count = lax.axis_size("dp")
    adapter_count = adapter_storage_slot.shape[0]
    compare = row_adapter_index[:, None] == jnp.arange(adapter_count, dtype=jnp.int32)[None, :]
    slot = jnp.sum(jnp.where(compare, adapter_storage_slot[None, :], 0), axis=1)
    pieces_a, pieces_b = (
        lax.all_gather(adapter_input_maps, "dp", axis=0, tiled=True),
        lax.all_gather(adapter_output_maps, "dp", axis=0, tiled=True),
    )
    pieces_a, pieces_b = (
        lax.all_to_all(pieces_a, "tensor", split_axis=2, concat_axis=0, tiled=True),
        lax.all_to_all(pieces_b, "tensor", split_axis=2, concat_axis=0, tiled=True),
    )
    position = slot % tensor_count * data_count + slot // tensor_count
    row_storage_slots = pieces_a.shape[0]
    rank_projection = pieces_a.shape[1]
    onehot = position[:, None] == jnp.arange(row_storage_slots, dtype=jnp.int32)[None, :]
    flattened_input_maps = pieces_a.reshape(row_storage_slots * rank_projection, pieces_a.shape[2])
    inner = lax.dot_general(
        hidden, flattened_input_maps, (((1,), (1,)), ((), ())), preferred_element_type=jnp.float32
    )
    low_part = jnp.sum(
        inner.reshape(-1, row_storage_slots, rank_projection)
        * onehot[:, :, None].astype(jnp.float32),
        axis=1,
    )
    low_b = lax.psum(low_part.astype(jnp.bfloat16), "tensor")
    widened_rows = (onehot[:, :, None].astype(jnp.bfloat16) * low_b[:, None, :]).reshape(
        -1, row_storage_slots * rank_projection
    )
    adapter_output = jnp.dot(
        widened_rows,
        pieces_b.reshape(row_storage_slots * rank_projection, pieces_b.shape[2]),
        preferred_element_type=jnp.float32,
    )
    partial_out = jnp.dot(hidden, down_matrix, preferred_element_type=jnp.float32)
    base = lax.psum_scatter(
        partial_out.astype(jnp.bfloat16), "tensor", scatter_dimension=1, tiled=True
    ).astype(jnp.float32)
    return (base + adapter_output).astype(jnp.bfloat16)


def solution(mesh):
    placed = (
        P(("groups", "dp"), "tensor"),
        P(("groups", "dp"), "tensor"),
        P("tensor", None),
        P(("dp", "tensor"), None, None),
        P(("dp", "tensor"), None, None),
        P(("groups", "dp")),
        P(),
    )
    sizes = dict(mesh.shape)
    fits = sizes["tensor"] == N_Y * N_Z and sizes["dp"] == 2 and sizes["groups"] == 2
    return jax.shard_map(
        local_fused if fits else local, mesh=mesh, in_specs=placed, out_specs=P(("groups", "dp"), "tensor"), check_vma=False
    )
```
